512 devices in a mesh: section: 8 (over y, z_hi), replica: 64 (over z_lo, x, core).
Axes of the slice: x: 4, y: 4, z: 16 (z_hi: 2, z_lo: 8; z = z_hi * 8 + z_lo), core: 2. Of those that a mesh axis runs over, the one named last changes fastest.
Arguments:
- embeds: bfloat16 [8192, 4096], P('replica'), may hold values from -16 to 16
- shared_basis: bfloat16 [4096, 256], replicated, as said below
- down_proj: bfloat16 [8, 4096, 64], P('section'), may hold values from -0.09375 to 0.09375
- up_proj: bfloat16 [8, 4096, 64], P('section'), may hold values from -0.75 to 0.75
- norm_gain: float32 [8, 4096], P('section'), may hold values from 0.1 to 1.9
- coef_grad: bfloat16 [8192, 256], P('replica'), may hold values from -0.15625 to 0.15625
Outputs:
- coefs: bfloat16 [8, 8192, 256], P('section', 'replica')
- weight_grads: float32 [8, 4096, 128], P('section', 'replica')
The draws below stay inside these ranges and needn't reach their ends.
Inputs may be any that keep to these rules, and one draw needn't show every extreme that they name: The columns of shared_basis are orthonormal up to bfloat16 rounding.
All inputs are finite; a program needn't handle non-finite values.
Results may differ from the reference program's by a relative error of at most 0.014.
Values may be sent and summed in bfloat16 or wider, within the bound.
No kernel may reach another device: no remote copies, remote signals or barrier semaphores. Data moves between devices by JAX's collectives and lax.ppermute only.
A program may use at most 64 MiB of HBM per device.

```python
import jax
import jax.numpy as jnp
from jax import lax

D = 4096
R = 256
K = 64
TOKENS = 8192
N_SECTION = 8


def draw_shared_basis(key, part):
    key = jax.random.fold_in(key, 11)
    perm_key, sign_key = jax.random.split(key)
    group_rows = D // R
    row_order = jax.random.permutation(perm_key, D).astype(jnp.int32)
    column_of_row = row_order // group_rows
    columns = jnp.arange(R, dtype=jnp.int32)
    picked = (column_of_row[:, None] == columns[None, :]).astype(jnp.float32)
    sign_bits = jax.random.randint(sign_key, (D,), 0, 2).astype(jnp.float32)
    row_signs = 2.0 * sign_bits - 1.0
    magnitude = jnp.float32(group_rows) ** (-0.5)
    return (picked * row_signs[:, None] * magnitude).astype(jnp.bfloat16)


def strengthened(drawn, rng, source, target, shards_of, factor):
    def block_of(dim):
        return (jnp.arange(drawn.shape[dim]) // (drawn.shape[dim] // shards_of)).reshape((-1,) + (1,) * (drawn.ndim - 1 - dim))

    near = jax.random.permutation(rng, shards_of)[block_of(target)]
    other_side = (block_of(target) + shards_of // 2) % shards_of
    return jnp.where((block_of(source) == near) | (block_of(source) == other_side), factor * drawn, drawn)


def level_of(stream_key, dims, cuts, low, top_value):
    level, own = 1.0, jax.random.fold_in(stream_key, 6)
    for position, parts in cuts:
        heights = jnp.exp(jax.random.uniform(jax.random.fold_in(own, position), (parts,), jnp.float32, low / len(cuts), top_value / len(cuts)))
        level = level * jnp.repeat(heights, dims[position] // parts).reshape([-1 if axis == position else 1 for axis in range(len(dims))])
    return level


def scatter_about(rng, shape, width, limit, shards=(), held_as=jnp.bfloat16):
    array = width * jax.random.normal(rng, shape, jnp.float32)
    if shards:
        array = array * level_of(rng, shape, shards, -0.22, 0.18)
    return jnp.clip(array, -limit, limit).astype(held_as)


def heavy_noise(rng, dims, deviation, reach, cuts, heavy, held_as=jnp.bfloat16):
    values = deviation * jax.random.normal(rng, dims, jnp.float32)
    if cuts:
        values = values * level_of(rng, dims, cuts, -0.22, 0.18)
    return jnp.clip(strengthened(values, jax.random.fold_in(rng, 3), *heavy), -reach, reach).astype(held_as)


def setup_inputs(seed: int = 0) -> dict:
    streams_of = jax.random.split(jax.random.key(seed), 7)
    return {
        "embeds": heavy_noise(streams_of[0], (TOKENS, D), 1.0, 16.0, ((0, 64),), (0, 1, 64, 4.0)),
        "shared_basis": draw_shared_basis(jax.random.fold_in(streams_of[6], 71), 0),
        "down_proj": scatter_about(streams_of[2], (N_SECTION, D, K), D ** -0.5, 0.09375, ((0, 8),)),
        "up_proj": scatter_about(streams_of[3], (N_SECTION, D, K), K ** -0.5, 0.75, ((0, 8),)),
        "norm_gain": jnp.clip(1.0 + 0.18 * jax.random.normal(streams_of[4], (N_SECTION, D), jnp.float32), 0.1, 1.9),
        "coef_grad": scatter_about(streams_of[5], (TOKENS, R), (TOKENS ** -0.5), 0.15625, ((0, 64),)),
    }


eps_norm = 1e-05

def section_forward(coef_in, embedded, basis, down_weight, up_weight, gain_row):
    expanded = jnp.dot(coef_in, basis.T, preferred_element_type=jnp.float32)
    hidden = embedded.astype(jnp.float32) + expanded
    inverse_rms = lax.rsqrt(lax.optimization_barrier(jnp.mean(hidden * hidden, axis=-1, keepdims=True)) + eps_norm)
    normed = (hidden * inverse_rms * gain_row).astype(jnp.bfloat16)
    preact = jnp.dot(normed, down_weight, preferred_element_type=jnp.float32)
    activation = jax.nn.silu(preact).astype(jnp.bfloat16)
    branch = jnp.dot(activation, up_weight.T, preferred_element_type=jnp.float32)
    delta_rows = (expanded + branch).astype(jnp.bfloat16)
    coef_out = jnp.dot(delta_rows, basis, preferred_element_type=jnp.float32).astype(jnp.bfloat16)
    return (coef_out, hidden, inverse_rms, normed, preact, activation)

def section_backward(grad_out, hidden, inverse_rms, normed, preact, activation, basis, down_weight, up_weight, gain_row):
    grad_delta = jnp.dot(grad_out, basis.T, preferred_element_type=jnp.float32).astype(jnp.bfloat16)
    grad_act = jnp.dot(grad_delta, up_weight, preferred_element_type=jnp.float32)
    sigmoid_pre = jax.nn.sigmoid(preact)
    grad_pre = (grad_act * sigmoid_pre * (1.0 + preact * (1.0 - sigmoid_pre))).astype(jnp.bfloat16)
    grad_normed = jnp.dot(grad_pre, down_weight.T, preferred_element_type=jnp.float32)
    scaled_rows = hidden * inverse_rms
    grad_scaled = grad_normed * gain_row
    grad_hidden = inverse_rms * (grad_scaled - scaled_rows * lax.optimization_barrier(jnp.mean(grad_scaled * scaled_rows, axis=-1, keepdims=True)))
    grad_base = (grad_delta.astype(jnp.float32) + grad_hidden).astype(jnp.bfloat16)
    grad_in = jnp.dot(grad_base, basis, preferred_element_type=jnp.float32).astype(jnp.bfloat16)
    weight_rows = jnp.concatenate([jnp.dot(normed.T, grad_pre, preferred_element_type=jnp.float32), jnp.dot(grad_delta.T, activation, preferred_element_type=jnp.float32)], axis=1)
    return (grad_in, weight_rows)

def reference(embeds, shared_basis, down_proj, up_proj, norm_gain, coef_grad):
    coef_in = jnp.zeros((embeds.shape[0], shared_basis.shape[1]), jnp.bfloat16)
    inputs_kept = []
    outputs_kept = []
    for section_index in range(N_SECTION):
        inputs_kept.append(coef_in)
        coef_in = section_forward(coef_in, embeds, shared_basis, down_proj[section_index], up_proj[section_index], norm_gain[section_index])[0]
        outputs_kept.append(coef_in)
    grad_out = coef_grad
    grads_kept = [None] * N_SECTION
    for section_index in reversed(range(N_SECTION)):
        saved = section_forward(inputs_kept[section_index], embeds, shared_basis, down_proj[section_index], up_proj[section_index], norm_gain[section_index])
        grad_out, grads_kept[section_index] = section_backward(grad_out, saved[1], saved[2], saved[3], saved[4], saved[5], shared_basis, down_proj[section_index], up_proj[section_index], norm_gain[section_index])
    return (jnp.stack(outputs_kept), jnp.stack(grads_kept))
```

```python
import functools

import jax
import jax.numpy as jnp
from jax import lax
from jax.experimental import pallas as pl
from jax.experimental.pallas import tpu as pltpu
from jax.sharding import Mesh, PartitionSpec as P

F32 = jnp.float32
BF16 = jnp.bfloat16
EPS = 1e-05
SECTION = ("y", "z_hi")
REPLICA = ("z_lo", "x", "core")
AXES = SECTION + REPLICA
SIZES = (4, 2, 8, 4, 2)

NN = (((1,), (0,)), ((), ()))
NT = (((1,), (1,)), ((), ()))
TN = (((0,), (0,)), ((), ()))


def dot(a, b, dims=NN):
    return lax.dot_general(a, b, dims, preferred_element_type=F32)


def project_kernel(steps, emb, basis, down, up, gain, block, emb_basis, norm, acc, acc_pre):
    step = pl.program_id(0)
    e = emb[...]
    down_t = (down[...].astype(F32).T * gain[...]).astype(BF16)
    up_t = up[...].astype(F32).T.astype(BF16)
    stacked = jnp.concatenate([e, down_t, up_t], axis=0)
    part = dot(stacked, basis[...])
    pre = dot(e, down_t, NT)
    ef = e.astype(F32)
    sq = ef * ef
    width = sq.shape[1]
    square = sq[:, :128]
    for at in range(128, width, 128):
        square = square + sq[:, at : at + 128]

    @pl.when(step == 0)
    def _():
        acc[...] = part
        acc_pre[...] = pre
        norm[...] = square

    @pl.when(step > 0)
    def _():
        acc[...] += part
        acc_pre[...] += pre
        norm[...] += square

    @pl.when(step == steps - 1)
    def _():
        rows = emb_basis.shape[0]
        emb_basis[...] = acc[:rows, :]
        block[:, :256] = acc[rows:, :].astype(BF16)
        total = acc_pre[...]
        high = total.astype(BF16)
        block[:, 256:320] = high
        block[:, 320:384] = (total - high.astype(F32)).astype(BF16)
        norm[...] = jnp.broadcast_to(jnp.sum(norm[...], axis=1, keepdims=True), norm.shape)


def project(embeds, basis, down, up, gain):
    rows, width = embeds.shape
    rank = basis.shape[1]
    inner = down.shape[1]
    steps = 8
    chunk = width // steps
    return pl.pallas_call(
        functools.partial(project_kernel, steps),
        grid=(steps,),
        in_specs=[
            pl.BlockSpec((rows, chunk), lambda i: (0, i)),
            pl.BlockSpec((chunk, rank), lambda i: (i, 0)),
            pl.BlockSpec((chunk, inner), lambda i: (i, 0)),
            pl.BlockSpec((chunk, inner), lambda i: (i, 0)),
            pl.BlockSpec((1, chunk), lambda i: (0, i)),
        ],
        out_specs=[
            pl.BlockSpec((2 * inner, rank + 2 * inner), lambda i: (0, 0)),
            pl.BlockSpec((rows, rank), lambda i: (0, 0)),
            pl.BlockSpec((rows, 128), lambda i: (0, 0)),
        ],
        out_shape=[
            jax.ShapeDtypeStruct((2 * inner, rank + 2 * inner), BF16),
            jax.ShapeDtypeStruct((rows, rank), F32),
            jax.ShapeDtypeStruct((rows, 128), F32),
        ],
        scratch_shapes=[
            pltpu.VMEM((rows + 2 * inner, rank), F32),
            pltpu.VMEM((rows, inner), F32),
        ],
        compiler_params=pltpu.CompilerParams(vmem_limit_bytes=32 * 1024 * 1024),
        name="project",
    )(embeds, basis, down, up, gain)


def chain_kernel(
    count, place, blocks, emb_basis, norm, cotangent, emb, basis, gain,
    coefs, slots, c_kept, g_kept, p_kept, a_kept, pre_kept, slope_kept, inv_kept, wide,
):
    width = emb.shape[1]
    inner = 64
    eu = emb_basis[...]
    sq = norm[:, :1]
    c = jnp.zeros(eu.shape, BF16)
    c_kept[0] = c
    for s in range(count):
        cf = c.astype(F32)
        pre = blocks[s, :, 256:320].astype(F32) + blocks[s, :, 320:384].astype(F32)
        total = sq
        if s:
            pre = pre + dot(c, blocks[s, :inner, :256], NT)
            total = total + jnp.sum(cf * (2.0 * eu + cf), axis=1, keepdims=True)
        inv = lax.rsqrt(jnp.maximum(total, 0.0) * (1.0 / width) + EPS)
        pre = pre * inv
        sig = 1.0 / (1.0 + jnp.exp(-pre))
        act = (pre * sig).astype(BF16)
        pre_kept[s] = pre
        slope_kept[s] = sig * (1.0 + pre * (1.0 - sig))
        inv_kept[s] = jnp.broadcast_to(inv, inv_kept.shape[1:])
        a_kept[s] = act
        c = (cf + dot(act, blocks[s, inner:, :256])).astype(BF16)
        c_kept[s + 1] = c

    g = cotangent[...]
    for s in reversed(range(count)):
        g_kept[s] = g
        inv = inv_kept[s][:, :1]
        gp = (dot(g, blocks[s, inner:, :256], NT) * slope_kept[s]).astype(BF16)
        gpf = gp.astype(F32)
        p_kept[s] = gpf * inv
        if s:
            mean = jnp.sum(gpf * pre_kept[s], axis=1, keepdims=True) * (1.0 / width)
            back = dot(gp, blocks[s, :inner, :256])
            hid = eu + c_kept[s].astype(F32)
            g = (g.astype(F32) + inv * back - (inv * inv * mean) * hid).astype(BF16)

    me = place[0]
    coefs[...] = c_kept[me + 1]
    p_t = p_kept[me].T.astype(BF16)
    cp = dot(p_t, c_kept[me]).astype(BF16)
    act_t = a_kept[me].astype(F32).T.astype(BF16)
    s2 = dot(act_t, g_kept[me]).astype(BF16)
    for at in range(0, width, 1024):
        cols = slice(at, at + 1024)
        grad = dot(p_t, emb[:, cols]) + dot(cp, basis[cols, :], NT)
        wide[:, cols] = grad * gain[:, cols]
    low = lax.broadcasted_iota(jnp.int32, (inner, 128), 1) < 64
    for x in range(4):
        for q in range(4):
            first = wide[:, ((2 * q) * 4 + x) * 128 : ((2 * q) * 4 + x) * 128 + 128]
            second = wide[:, ((2 * q + 1) * 4 + x) * 128 : ((2 * q + 1) * 4 + x) * 128 + 128]
            lanes = slice(q * 128, q * 128 + 128)
            slots[2 * x, :, lanes] = jnp.where(low, first, pltpu.roll(second, 64, 1)).astype(BF16)
            slots[2 * x + 1, :, lanes] = jnp.where(low, pltpu.roll(first, 64, 1), second).astype(BF16)
    for j in range(8):
        slots[j, :, 512:768] = s2


def chain(place, blocks, emb_basis, norm, cotangent, embeds, basis, gain):
    count = blocks.shape[0]
    rows, rank = cotangent.shape
    inner = 64
    width = embeds.shape[1]
    vmem = pl.BlockSpec(memory_space=pltpu.VMEM)
    return pl.pallas_call(
        functools.partial(chain_kernel, count),
        in_specs=[pl.BlockSpec(memory_space=pltpu.SMEM)] + [vmem] * 7,
        out_specs=[vmem, vmem],
        out_shape=[
            jax.ShapeDtypeStruct((rows, rank), BF16),
            jax.ShapeDtypeStruct((8, inner, 768), BF16),
        ],
        scratch_shapes=[
            pltpu.VMEM((count + 1, rows, rank), BF16),
            pltpu.VMEM((count, rows, rank), BF16),
            pltpu.VMEM((count, rows, inner), F32),
            pltpu.VMEM((count, rows, inner), BF16),
            pltpu.VMEM((count, rows, inner), F32),
            pltpu.VMEM((count, rows, inner), F32),
            pltpu.VMEM((count, rows, 128), F32),
            pltpu.VMEM((inner, width), F32),
        ],
        compiler_params=pltpu.CompilerParams(vmem_limit_bytes=32 * 1024 * 1024),
        name="chain",
    )(place, blocks, emb_basis, norm, cotangent, embeds, basis, gain)


def middle_kernel(place, got, basis, out):
    total = got[0].astype(F32)
    for j in range(1, got.shape[0]):
        total = total + got[j].astype(F32)
    rows = basis[:, 0].reshape(512, 256)
    w2 = dot(total[:, 512:].astype(BF16), rows, NT)
    both = jnp.concatenate([total[:, :512], w2], axis=0)
    out[...] = both.T.astype(BF16).reshape(out.shape)


def middle(place, got, basis):
    view = basis.reshape(8, 8, 64, 256)
    return pl.pallas_call(
        middle_kernel,
        grid_spec=pltpu.PrefetchScalarGridSpec(
            num_scalar_prefetch=1,
            grid=(1,),
            in_specs=[
                pl.BlockSpec((8, 64, 768), lambda i, place: (0, 0, 0)),
                pl.BlockSpec((8, 1, 64, 256), lambda i, place: (0, place[0], 0, 0)),
            ],
            out_specs=pl.BlockSpec((8, 64, 128), lambda i, place: (0, 0, 0)),
        ),
        out_shape=jax.ShapeDtypeStruct((8, 64, 128), BF16),
        compiler_params=pltpu.CompilerParams(vmem_limit_bytes=32 * 1024 * 1024),
        name="middle",
    )(place, got, view)


def final_kernel(got, out):
    total = got[0].astype(F32)
    for j in range(1, got.shape[0]):
        total = total + got[j].astype(F32)
    out[...] = total


def final(got):
    return pl.pallas_call(
        final_kernel,
        out_shape=jax.ShapeDtypeStruct(got.shape[1:], F32),
        name="final",
    )(got)


def gather_sections(block):
    other = lax.ppermute(block, "z_hi", [(0, 1), (1, 0)])
    mine = lax.axis_index("z_hi")
    pair = jnp.where(mine == 0, jnp.stack([block, other]), jnp.stack([other, block]))
    every = lax.all_gather(pair, "y", tiled=False)
    return every.reshape((8,) + block.shape)


def local(embeds, shared_basis, down_proj, up_proj, norm_gain, coef_grad):
    place = lax.axis_index(SECTION).astype(jnp.int32).reshape(1)
    lane = lax.axis_index(("x", "core")).astype(jnp.int32).reshape(1)
    block, emb_basis, norm = project(embeds, shared_basis, down_proj[0], up_proj[0], norm_gain)
    blocks = gather_sections(block)
    coefs, slots = chain(place, blocks, emb_basis, norm, coef_grad, embeds, shared_basis, norm_gain)
    got = lax.all_to_all(slots, ("x", "core"), 0, 0, tiled=True)
    summed = middle(lane, got, shared_basis)
    got = lax.all_to_all(summed, "z_lo", 0, 0, tiled=True)
    return coefs[None], final(got)[None]


def solution(mesh):
    fine = Mesh(mesh.devices.reshape(SIZES), AXES)
    placed = (
        P(REPLICA, None),
        P(),
        P(SECTION, None, None),
        P(SECTION, None, None),
        P(SECTION, None),
        P(REPLICA, None),
    )
    return jax.shard_map(
        local,
        mesh=fine,
        in_specs=placed,
        out_specs=(P(SECTION, REPLICA, None), P(SECTION, REPLICA, None)),
        check_vma=False,
    )
```

```python
import functools

import jax
import jax.numpy as jnp
from jax import lax
from jax.experimental import pallas as pl
from jax.experimental.pallas import tpu as pltpu
from jax.sharding import Mesh, PartitionSpec as P

F32 = jnp.float32
BF16 = jnp.bfloat16
EPS = 1e-05
SECTION = ("y", "z_hi")
REPLICA = ("z_lo", "x", "core")
AXES = SECTION + REPLICA
SIZES = (4, 2, 8, 4, 2)

NN = (((1,), (0,)), ((), ()))
NT = (((1,), (1,)), ((), ()))
TN = (((0,), (0,)), ((), ()))


def dot(a, b, dims=NN):
    return lax.dot_general(a, b, dims, preferred_element_type=F32)


def project_kernel(
    chunk, emb_hbm, basis_hbm, down_hbm, up_hbm, gain_hbm,
    block, repeated, emb_basis, norm, emb, basis, down, up, gain, sems,
):
    rows, width = emb.shape
    steps = width // chunk
    gain_copy = pltpu.make_async_copy(gain_hbm, gain, sems.at[4, 0])
    gain_copy.start()
    copies = []
    for i in range(steps):
        at = slice(i * chunk, (i + 1) * chunk)
        group = [
            pltpu.make_async_copy(down_hbm.at[:, at], down.at[:, at], sems.at[0, i]),
            pltpu.make_async_copy(up_hbm.at[:, at], up.at[:, at], sems.at[1, i]),
            pltpu.make_async_copy(emb_hbm.at[:, at], emb.at[:, at], sems.at[2, i]),
            pltpu.make_async_copy(basis_hbm.at[at, :], basis.at[at, :], sems.at[3, i]),
        ]
        for copy in group:
            copy.start()
        copies.append(group)
    gain_copy.wait()
    acc = jnp.zeros((rows + 128, basis.shape[1]), F32)
    acc_pre = jnp.zeros((rows, 64), F32)
    square = jnp.zeros((rows, 128), F32)
    for i in range(steps):
        at = slice(i * chunk, (i + 1) * chunk)
        for copy in copies[i]:
            copy.wait()
        e = emb[:, at]
        scaled = (down[:, at].astype(F32) * gain[:, at]).astype(BF16)
        stacked = jnp.concatenate([e, scaled, up[:, at]], axis=0)
        acc = acc + dot(stacked, basis[at, :])
        acc_pre = acc_pre + dot(e, scaled, NT)
        ef = e.astype(F32)
        sq = ef * ef
        for k in range(0, chunk, 128):
            square = square + sq[:, k : k + 128]
    emb_basis[...] = acc[:rows, :]
    high = acc_pre.astype(BF16)
    low = (acc_pre - high.astype(F32)).astype(BF16)
    weights = acc[rows:, :].astype(BF16)
    for ref in (block, repeated.at[0], repeated.at[1], repeated.at[2], repeated.at[3]):
        ref[:, :256] = weights
        ref[:, 256:320] = high
        ref[:, 320:384] = low
    norm[...] = jnp.broadcast_to(jnp.sum(square, axis=1, keepdims=True), norm.shape)


def project(embeds, basis, down_t, up_t, gain):
    rows, width = embeds.shape
    rank = basis.shape[1]
    inner = down_t.shape[0]
    chunk = 512
    hbm = pl.BlockSpec(memory_space=pltpu.HBM)
    vmem = pl.BlockSpec(memory_space=pltpu.VMEM)
    return pl.pallas_call(
        functools.partial(project_kernel, chunk),
        in_specs=[hbm] * 5,
        out_specs=[vmem] * 4,
        out_shape=[
            jax.ShapeDtypeStruct((2 * inner, rank + 2 * inner), BF16),
            jax.ShapeDtypeStruct((4, 2 * inner, rank + 2 * inner), BF16),
            jax.ShapeDtypeStruct((rows, rank), F32),
            jax.ShapeDtypeStruct((rows, 128), F32),
        ],
        scratch_shapes=[
            pltpu.VMEM((rows, width), BF16),
            pltpu.VMEM((width, rank), BF16),
            pltpu.VMEM((inner, width), BF16),
            pltpu.VMEM((inner, width), BF16),
            pltpu.VMEM((1, width), F32),
            pltpu.SemaphoreType.DMA((5, width // chunk)),
        ],
        compiler_params=pltpu.CompilerParams(vmem_limit_bytes=60 * 1024 * 1024),
        name="project",
    )(embeds, basis, down_t, up_t, gain)


def chain_kernel(
    count, place, own, other, emb_basis, norm, cotangent, emb, basis, gain,
    coefs, slots_out, blocks, c_kept, g_kept, p_kept, a_kept, pre_kept, slope_kept, inv_kept, wide, slots, sems,
):
    width = emb.shape[1]
    inner = 64
    half = place[1]
    for y in range(count // 2):
        blocks[2 * y + half] = own[y]
        blocks[2 * y + 1 - half] = other[y]
    eu = emb_basis[...]
    sq = norm[:, :1]
    c = jnp.zeros(eu.shape, BF16)
    c_kept[0] = c
    for s in range(count):
        cf = c.astype(F32)
        pre = blocks[s, :, 256:320].astype(F32) + blocks[s, :, 320:384].astype(F32)
        total = sq
        if s:
            pre = pre + dot(c, blocks[s, :inner, :256], NT)
            total = total + jnp.sum(cf * (2.0 * eu + cf), axis=1, keepdims=True)
        inv = lax.rsqrt(jnp.maximum(total, 0.0) * (1.0 / width) + EPS)
        pre = pre * inv
        sig = 1.0 / (1.0 + jnp.exp(-pre))
        act = (pre * sig).astype(BF16)
        pre_kept[s] = pre
        slope_kept[s] = sig * (1.0 + pre * (1.0 - sig))
        inv_kept[s] = jnp.broadcast_to(inv, inv_kept.shape[1:])
        a_kept[s] = act
        c = (cf + dot(act, blocks[s, inner:, :256])).astype(BF16)
        c_kept[s + 1] = c

    g = cotangent[...]
    for s in reversed(range(count)):
        g_kept[s] = g
        inv = inv_kept[s][:, :1]
        gp = (dot(g, blocks[s, inner:, :256], NT) * slope_kept[s]).astype(BF16)
        gpf = gp.astype(F32)
        p_kept[s] = gpf * inv
        if s:
            mean = jnp.sum(gpf * pre_kept[s], axis=1, keepdims=True) * (1.0 / width)
            back = dot(gp, blocks[s, :inner, :256])
            hid = eu + c_kept[s].astype(F32)
            g = (g.astype(F32) + inv * back - (inv * inv * mean) * hid).astype(BF16)

    me = place[0]
    coefs[...] = c_kept[me + 1]
    p_t = p_kept[me].T.astype(BF16)
    cp = dot(p_t, c_kept[me]).astype(BF16)
    act_t = a_kept[me].astype(F32).T.astype(BF16)
    s2 = dot(act_t, g_kept[me]).astype(BF16)
    for at in range(0, width, 1024):
        cols = slice(at, at + 1024)
        grad = dot(p_t, emb[:, cols]) + dot(cp, basis[cols, :], NT)
        wide[:, cols] = grad * gain[:, cols]
    low = lax.broadcasted_iota(jnp.int32, (inner, 128), 1) < 64
    copies = [pltpu.make_async_copy(slots.at[j], slots_out.at[j], sems.at[j]) for j in range(8)]
    for x in range(4):
        for q in range(4):
            first = wide[:, ((2 * q) * 4 + x) * 128 : ((2 * q) * 4 + x) * 128 + 128]
            second = wide[:, ((2 * q + 1) * 4 + x) * 128 : ((2 * q + 1) * 4 + x) * 128 + 128]
            lanes = slice(q * 128, q * 128 + 128)
            slots[2 * x, :, lanes] = jnp.where(low, first, pltpu.roll(second, 64, 1)).astype(BF16)
            slots[2 * x + 1, :, lanes] = jnp.where(low, pltpu.roll(first, 64, 1), second).astype(BF16)
        for j in (2 * x, 2 * x + 1):
            slots[j, :, 512:768] = s2
            copies[j].start()
    for copy in copies:
        copy.wait()


def chain(place, own, other, emb_basis, norm, cotangent, embeds, basis, gain):
    count = 2 * own.shape[0]
    rows, rank = cotangent.shape
    inner = 64
    width = embeds.shape[1]
    vmem = pl.BlockSpec(memory_space=pltpu.VMEM)
    return pl.pallas_call(
        functools.partial(chain_kernel, count),
        in_specs=[pl.BlockSpec(memory_space=pltpu.SMEM)] + [vmem] * 8,
        out_specs=[vmem, pl.BlockSpec(memory_space=pltpu.HBM)],
        out_shape=[
            jax.ShapeDtypeStruct((rows, rank), BF16),
            jax.ShapeDtypeStruct((8, inner, 768), BF16),
        ],
        scratch_shapes=[
            pltpu.VMEM((count,) + own.shape[1:], BF16),
            pltpu.VMEM((count + 1, rows, rank), BF16),
            pltpu.VMEM((count, rows, rank), BF16),
            pltpu.VMEM((count, rows, inner), F32),
            pltpu.VMEM((count, rows, inner), BF16),
            pltpu.VMEM((count, rows, inner), F32),
            pltpu.VMEM((count, rows, inner), F32),
            pltpu.VMEM((count, rows, 128), F32),
            pltpu.VMEM((inner, width), F32),
            pltpu.VMEM((8, inner, 768), BF16),
            pltpu.SemaphoreType.DMA((8,)),
        ],
        compiler_params=pltpu.CompilerParams(vmem_limit_bytes=32 * 1024 * 1024),
        name="chain",
    )(place, own, other, emb_basis, norm, cotangent, embeds, basis, gain)


def middle_kernel(place, got, basis, out):
    total = got[0].astype(F32)
    for j in range(1, got.shape[0]):
        total = total + got[j].astype(F32)
    rows = basis[:, 0].reshape(512, 256)
    w2 = dot(total[:, 512:].astype(BF16), rows, NT)
    both = jnp.concatenate([total[:, :512], w2], axis=0)
    out[...] = both.T.astype(BF16).reshape(out.shape)


def middle(place, got, basis):
    view = basis.reshape(8, 8, 64, 256)
    return pl.pallas_call(
        middle_kernel,
        grid_spec=pltpu.PrefetchScalarGridSpec(
            num_scalar_prefetch=1,
            grid=(1,),
            in_specs=[
                pl.BlockSpec((8, 64, 768), lambda i, place: (0, 0, 0)),
                pl.BlockSpec((8, 1, 64, 256), lambda i, place: (0, place[0], 0, 0)),
            ],
            out_specs=pl.BlockSpec((8, 64, 128), lambda i, place: (0, 0, 0)),
        ),
        out_shape=jax.ShapeDtypeStruct((8, 64, 128), BF16),
        compiler_params=pltpu.CompilerParams(vmem_limit_bytes=32 * 1024 * 1024),
        name="middle",
    )(place, got, view)


def final_kernel(got, out):
    total = got[0].astype(F32)
    for j in range(1, got.shape[0]):
        total = total + got[j].astype(F32)
    out[...] = total


def final(got):
    return pl.pallas_call(
        final_kernel,
        out_shape=jax.ShapeDtypeStruct(got.shape[1:], F32),
        name="final",
    )(got)


def local(embeds, shared_basis, down_proj, up_proj, norm_gain, coef_grad):
    half = lax.axis_index("z_hi")
    place = jnp.stack([2 * lax.axis_index("y") + half, half]).astype(jnp.int32)
    lane = lax.axis_index(("x", "core")).astype(jnp.int32).reshape(1)
    block, repeated, emb_basis, norm = project(
        embeds, shared_basis, down_proj[0].T, up_proj[0].T, norm_gain
    )
    crossed = lax.ppermute(block, "z_hi", [(0, 1), (1, 0)])
    own = lax.all_to_all(repeated, "y", 0, 0, tiled=True)
    crossed = jnp.broadcast_to(crossed[None], repeated.shape)
    other = lax.all_to_all(crossed, "y", 0, 0, tiled=True)
    coefs, slots = chain(place, own, other, emb_basis, norm, coef_grad, embeds, shared_basis, norm_gain)
    got = lax.all_to_all(slots, ("x", "core"), 0, 0, tiled=True)
    summed = middle(lane, got, shared_basis)
    got = lax.all_to_all(summed, "z_lo", 0, 0, tiled=True)
    return coefs[None], final(got)[None]


def solution(mesh):
    fine = Mesh(mesh.devices.reshape(SIZES), AXES)
    placed = (
        P(REPLICA, None),
        P(),
        P(SECTION, None, None),
        P(SECTION, None, None),
        P(SECTION, None),
        P(REPLICA, None),
    )
    return jax.shard_map(
        local,
        mesh=fine,
        in_specs=placed,
        out_specs=(P(SECTION, REPLICA, None), P(SECTION, REPLICA, None)),
        check_vma=False,
    )
```

```python
import functools

import jax
import jax.numpy as jnp
from jax import lax
from jax.experimental import pallas as pl
from jax.experimental.pallas import tpu as pltpu
from jax.sharding import Mesh, PartitionSpec as P

F32 = jnp.float32
BF16 = jnp.bfloat16
EPS = 1e-05
SECTION = ("y", "z_hi")
REPLICA = ("z_lo", "x", "core")
AXES = SECTION + REPLICA
SIZES = (4, 2, 8, 4, 2)

NN = (((1,), (0,)), ((), ()))
NT = (((1,), (1,)), ((), ()))
TN = (((0,), (0,)), ((), ()))


def dot(a, b, dims=NN):
    return lax.dot_general(a, b, dims, preferred_element_type=F32)


def project_kernel(
    chunk, emb_hbm, basis_hbm, down_hbm, up_hbm, gain_hbm,
    block, emb_basis, norm, emb, basis, down, up, gain, sems,
):
    rows, width = emb.shape
    steps = width // chunk
    gain_copy = pltpu.make_async_copy(gain_hbm, gain, sems.at[4, 0])
    gain_copy.start()
    copies = []
    for i in range(steps):
        at = slice(i * chunk, (i + 1) * chunk)
        group = [
            pltpu.make_async_copy(down_hbm.at[:, at], down.at[:, at], sems.at[0, i]),
            pltpu.make_async_copy(up_hbm.at[:, at], up.at[:, at], sems.at[1, i]),
            pltpu.make_async_copy(emb_hbm.at[:, at], emb.at[:, at], sems.at[2, i]),
            pltpu.make_async_copy(basis_hbm.at[at, :], basis.at[at, :], sems.at[3, i]),
        ]
        for copy in group:
            copy.start()
        copies.append(group)
    gain_copy.wait()
    acc = jnp.zeros((rows + 128, basis.shape[1]), F32)
    acc_pre = jnp.zeros((rows, 64), F32)
    square = jnp.zeros((rows, 128), F32)
    for i in range(steps):
        at = slice(i * chunk, (i + 1) * chunk)
        for copy in copies[i]:
            copy.wait()
        e = emb[:, at]
        scaled = (down[:, at].astype(F32) * gain[:, at]).astype(BF16)
        stacked = jnp.concatenate([e, scaled, up[:, at]], axis=0)
        acc = acc + dot(stacked, basis[at, :])
        acc_pre = acc_pre + dot(e, scaled, NT)
        ef = e.astype(F32)
        sq = ef * ef
        for k in range(0, chunk, 128):
            square = square + sq[:, k : k + 128]
    emb_basis[...] = acc[:rows, :]
    high = acc_pre.astype(BF16)
    low = (acc_pre - high.astype(F32)).astype(BF16)
    weights = acc[rows:, :].astype(BF16)
    block[:, :256] = weights
    block[:, 256:320] = high
    block[:, 320:384] = low
    norm[...] = jnp.broadcast_to(jnp.sum(square, axis=1, keepdims=True), norm.shape)


def project(embeds, basis, down_t, up_t, gain):
    rows, width = embeds.shape
    rank = basis.shape[1]
    inner = down_t.shape[0]
    chunk = 512
    hbm = pl.BlockSpec(memory_space=pltpu.HBM)
    vmem = pl.BlockSpec(memory_space=pltpu.VMEM)
    args = [pltpu.with_memory_space_constraint(a, pltpu.HBM) for a in (embeds, basis, down_t, up_t, gain)]
    return pl.pallas_call(
        functools.partial(project_kernel, chunk),
        in_specs=[hbm] * 5,
        out_specs=[vmem] * 3,
        out_shape=[
            jax.ShapeDtypeStruct((2 * inner, rank + 2 * inner), BF16),
            jax.ShapeDtypeStruct((rows, rank), F32),
            jax.ShapeDtypeStruct((rows, 128), F32),
        ],
        scratch_shapes=[
            pltpu.VMEM((rows, width), BF16),
            pltpu.VMEM((width, rank), BF16),
            pltpu.VMEM((inner, width), BF16),
            pltpu.VMEM((inner, width), BF16),
            pltpu.VMEM((1, width), F32),
            pltpu.SemaphoreType.DMA((5, width // chunk)),
        ],
        compiler_params=pltpu.CompilerParams(vmem_limit_bytes=24 * 1024 * 1024),
        name="project",
    )(*args)


def chain_kernel(
    own, other, norm, emb_basis, cotangent, emb, basis, gain,
    coefs, slots_hbm,
    blocks, c_kept, g_kept, p_kept, a_kept, pre_kept, slope_kept, inv_kept, wide, slots, out_sems,
):
    count = blocks.shape[0] * blocks.shape[1]
    width = emb.shape[1]
    inner = 64
    half = lax.axis_index("z_hi")
    me = 2 * lax.axis_index("y") + half
    blocks[half] = own[...]
    blocks[1 - half] = other[...]

    def block_of(s):
        return blocks.at[s % 2, s // 2]

    eu = emb_basis[...]
    sq = norm[:, :1]
    c = jnp.zeros(eu.shape, BF16)
    c_kept[0] = c
    for s in range(count):
        block = block_of(s)
        cf = c.astype(F32)
        pre = block[:, 256:320].astype(F32) + block[:, 320:384].astype(F32)
        total = sq
        if s:
            pre = pre + dot(c, block[:inner, :256], NT)
            total = total + jnp.sum(cf * (2.0 * eu + cf), axis=1, keepdims=True)
        inv = lax.rsqrt(jnp.maximum(total, 0.0) * (1.0 / width) + EPS)
        pre = pre * inv
        sig = 1.0 / (1.0 + jnp.exp(-pre))
        act = (pre * sig).astype(BF16)
        pre_kept[s] = pre
        slope_kept[s] = sig * (1.0 + pre * (1.0 - sig))
        inv_kept[s] = jnp.broadcast_to(inv, inv_kept.shape[1:])
        a_kept[s] = act
        c = (cf + dot(act, block[inner:, :256])).astype(BF16)
        c_kept[s + 1] = c

    g = cotangent[...]
    for s in reversed(range(count)):
        block = block_of(s)
        g_kept[s] = g
        inv = inv_kept[s][:, :1]
        gp = (dot(g, block[inner:, :256], NT) * slope_kept[s]).astype(BF16)
        gpf = gp.astype(F32)
        p_kept[s] = gpf * inv
        if s:
            mean = jnp.sum(gpf * pre_kept[s], axis=1, keepdims=True) * (1.0 / width)
            back = dot(gp, block[:inner, :256])
            hid = eu + c_kept[s].astype(F32)
            g = (g.astype(F32) + inv * back - (inv * inv * mean) * hid).astype(BF16)

    coefs[...] = c_kept[me + 1]
    p_t = p_kept[me].T.astype(BF16)
    cp = dot(p_t, c_kept[me]).astype(BF16)
    act_t = a_kept[me].astype(F32).T.astype(BF16)
    s2 = dot(act_t, g_kept[me]).astype(BF16)
    for at in range(0, width, 1024):
        cols = slice(at, at + 1024)
        grad = dot(p_t, emb[:, cols]) + dot(cp, basis[cols, :], NT)
        wide[:, cols] = grad * gain[:, cols]
    low = lax.broadcasted_iota(jnp.int32, (inner, 128), 1) < 64
    copies = [pltpu.make_async_copy(slots.at[j], slots_hbm.at[j], out_sems.at[j]) for j in range(8)]
    for x in range(4):
        for q in range(4):
            first = wide[:, ((2 * q) * 4 + x) * 128 : ((2 * q) * 4 + x) * 128 + 128]
            second = wide[:, ((2 * q + 1) * 4 + x) * 128 : ((2 * q + 1) * 4 + x) * 128 + 128]
            lanes = slice(q * 128, q * 128 + 128)
            slots[2 * x, :, lanes] = jnp.where(low, first, pltpu.roll(second, 64, 1)).astype(BF16)
            slots[2 * x + 1, :, lanes] = jnp.where(low, pltpu.roll(first, 64, 1), second).astype(BF16)
        for j in (2 * x, 2 * x + 1):
            slots[j, :, 512:768] = s2
            copies[j].start()
    for copy in copies:
        copy.wait()


def chain(own, other, norm, emb_basis, cotangent, embeds, basis, gain):
    count = 2 * own.shape[0]
    rows, rank = cotangent.shape
    inner = 64
    width = embeds.shape[1]
    hbm = pl.BlockSpec(memory_space=pltpu.HBM)
    vmem = pl.BlockSpec(memory_space=pltpu.VMEM)
    return pl.pallas_call(
        chain_kernel,
        in_specs=[vmem] * 8,
        out_specs=[vmem, hbm],
        out_shape=[
            jax.ShapeDtypeStruct((rows, rank), BF16),
            pltpu.HBM((8, inner, 768), BF16),
        ],
        scratch_shapes=[
            pltpu.VMEM((2,) + own.shape, BF16),
            pltpu.VMEM((count + 1, rows, rank), BF16),
            pltpu.VMEM((count, rows, rank), BF16),
            pltpu.VMEM((count, rows, inner), F32),
            pltpu.VMEM((count, rows, inner), BF16),
            pltpu.VMEM((count, rows, inner), F32),
            pltpu.VMEM((count, rows, inner), F32),
            pltpu.VMEM((count, rows, 128), F32),
            pltpu.VMEM((inner, width), F32),
            pltpu.VMEM((8, inner, 768), BF16),
            pltpu.SemaphoreType.DMA((8,)),
        ],
        compiler_params=pltpu.CompilerParams(vmem_limit_bytes=32 * 1024 * 1024),
        name="chain",
    )(own, other, norm, emb_basis, cotangent, embeds, basis, gain)


def middle_kernel(place, got, basis, out):
    total = got[0].astype(F32)
    for j in range(1, got.shape[0]):
        total = total + got[j].astype(F32)
    rows = basis[:, 0].reshape(512, 256)
    w2 = dot(total[:, 512:].astype(BF16), rows, NT)
    both = jnp.concatenate([total[:, :512], w2], axis=0)
    out[...] = both.T.astype(BF16).reshape(out.shape)


def middle(place, got, basis):
    view = basis.reshape(8, 8, 64, 256)
    return pl.pallas_call(
        middle_kernel,
        grid_spec=pltpu.PrefetchScalarGridSpec(
            num_scalar_prefetch=1,
            grid=(1,),
            in_specs=[
                pl.BlockSpec((8, 64, 768), lambda i, place: (0, 0, 0)),
                pl.BlockSpec((8, 1, 64, 256), lambda i, place: (0, place[0], 0, 0)),
            ],
            out_specs=pl.BlockSpec((8, 64, 128), lambda i, place: (0, 0, 0)),
        ),
        out_shape=jax.ShapeDtypeStruct((8, 64, 128), BF16),
        compiler_params=pltpu.CompilerParams(vmem_limit_bytes=32 * 1024 * 1024),
        name="middle",
    )(place, got, view)


def final_kernel(got, out):
    total = got[0].astype(F32)
    for j in range(1, got.shape[0]):
        total = total + got[j].astype(F32)
    out[...] = total


def final(got):
    return pl.pallas_call(
        final_kernel,
        out_shape=jax.ShapeDtypeStruct(got.shape[1:], F32),
        name="final",
    )(got)


def local(embeds, shared_basis, down_proj, up_proj, norm_gain, coef_grad):
    lane = lax.axis_index(("x", "core")).astype(jnp.int32).reshape(1)
    block, emb_basis, norm = project(
        embeds, shared_basis, down_proj[0].T, up_proj[0].T, norm_gain
    )
    crossed = lax.ppermute(block, "z_hi", [(0, 1), (1, 0)])
    own = lax.all_gather(block, "y", tiled=False)
    other = lax.all_gather(crossed, "y", tiled=False)
    coefs, slots = chain(own, other, norm, emb_basis, coef_grad, embeds, shared_basis, norm_gain)
    got = lax.all_to_all(slots, ("x", "core"), 0, 0, tiled=True)
    summed = middle(lane, got, shared_basis)
    got = lax.all_to_all(summed, "z_lo", 0, 0, tiled=True)
    return coefs[None], final(got)[None]


def solution(mesh):
    fine = Mesh(mesh.devices.reshape(SIZES), AXES)
    placed = (
        P(REPLICA, None),
        P(),
        P(SECTION, None, None),
        P(SECTION, None, None),
        P(SECTION, None),
        P(REPLICA, None),
    )
    return jax.shard_map(
        local,
        mesh=fine,
        in_specs=placed,
        out_specs=(P(SECTION, REPLICA, None), P(SECTION, REPLICA, None)),
        check_vma=False,
    )
```

```python
import functools

import jax
import jax.numpy as jnp
from jax import lax
from jax.experimental import pallas as pl
from jax.experimental.pallas import tpu as pltpu
from jax.sharding import Mesh, PartitionSpec as P

F32 = jnp.float32
BF16 = jnp.bfloat16
EPS = 1e-05
SECTION = ("y", "z_hi")
REPLICA = ("z_lo", "x", "core")
AXES = SECTION + REPLICA
SIZES = (4, 2, 8, 4, 2)

NN = (((1,), (0,)), ((), ()))
NT = (((1,), (1,)), ((), ()))
TN = (((0,), (0,)), ((), ()))


def dot(a, b, dims=NN):
    return lax.dot_general(a, b, dims, preferred_element_type=F32)


def project_kernel(
    chunk, emb_hbm, basis_hbm, down_hbm, up_hbm, gain_hbm,
    block, part, emb_basis, norm, emb, basis, down, up, gain, sems,
):
    rows, width = emb.shape
    steps = width // chunk
    gain_copy = pltpu.make_async_copy(gain_hbm, gain, sems.at[4, 0])
    gain_copy.start()
    copies = []
    for i in range(steps):
        at = slice(i * chunk, (i + 1) * chunk)
        group = [
            pltpu.make_async_copy(down_hbm.at[:, at], down.at[:, at], sems.at[0, i]),
            pltpu.make_async_copy(up_hbm.at[:, at], up.at[:, at], sems.at[1, i]),
            pltpu.make_async_copy(emb_hbm.at[:, at], emb.at[:, at], sems.at[2, i]),
            pltpu.make_async_copy(basis_hbm.at[at, :], basis.at[at, :], sems.at[3, i]),
        ]
        for copy in group:
            copy.start()
        copies.append(group)
    gain_copy.wait()
    acc = jnp.zeros((rows + 128, basis.shape[1]), F32)
    acc_pre = jnp.zeros((rows, 64), F32)
    square = jnp.zeros((rows, 128), F32)
    for i in range(steps):
        at = slice(i * chunk, (i + 1) * chunk)
        for copy in copies[i]:
            copy.wait()
        e = emb[:, at]
        scaled = (down[:, at].astype(F32) * gain[:, at]).astype(BF16)
        stacked = jnp.concatenate([e, scaled, up[:, at]], axis=0)
        acc = acc + dot(stacked, basis[at, :])
        acc_pre = acc_pre + dot(e, scaled, NT)
        ef = e.astype(F32)
        sq = ef * ef
        for k in range(0, chunk, 128):
            square = square + sq[:, k : k + 128]
    emb_basis[...] = acc[:rows, :].T
    high = acc_pre.astype(BF16)
    block[:, :256] = acc[rows:, :].astype(BF16)
    block[:, 256:320] = high
    block[:, 320:384] = (acc_pre - high.astype(F32)).astype(BF16)
    first = lax.axis_index("core") == 0
    weights = jnp.where(first, acc[rows : rows + 64, :], acc[rows + 64 :, :])
    part[:, :256] = weights.astype(BF16)
    part[:, 256:320] = high[:64]
    part[:, 320:384] = high[64:]
    norm[...] = jnp.sum(square.T, axis=0, keepdims=True)


def project(embeds, basis, down_t, up_t, gain):
    rows, width = embeds.shape
    rank = basis.shape[1]
    inner = down_t.shape[0]
    chunk = 512
    hbm = pl.BlockSpec(memory_space=pltpu.HBM)
    vmem = pl.BlockSpec(memory_space=pltpu.VMEM)
    args = [pltpu.with_memory_space_constraint(a, pltpu.HBM) for a in (embeds, basis, down_t, up_t, gain)]
    return pl.pallas_call(
        functools.partial(project_kernel, chunk),
        in_specs=[hbm] * 5,
        out_specs=[vmem] * 4,
        out_shape=[
            jax.ShapeDtypeStruct((2 * inner, rank + 2 * inner), BF16),
            jax.ShapeDtypeStruct((inner, rank + 2 * inner), BF16),
            jax.ShapeDtypeStruct((rank, rows), F32),
            jax.ShapeDtypeStruct((1, rows), F32),
        ],
        scratch_shapes=[
            pltpu.VMEM((rows, width), BF16),
            pltpu.VMEM((width, rank), BF16),
            pltpu.VMEM((inner, width), BF16),
            pltpu.VMEM((inner, width), BF16),
            pltpu.VMEM((1, width), F32),
            pltpu.SemaphoreType.DMA((5, width // chunk)),
        ],
        compiler_params=pltpu.CompilerParams(vmem_limit_bytes=24 * 1024 * 1024),
        name="project",
    )(*args)


def chain_kernel(
    own0, own1, own2, own3, other, norm, emb_basis, cotangent, emb, basis, gain,
    coefs_hbm, slots,
    weights, turned, pre_emb, c_kept, g_kept, p_kept, a_kept, pre_kept, slope_kept, coefs, coefs_sem,
):
    count = weights.shape[0]
    width = emb.shape[1]
    inner = 64
    half = lax.axis_index("z_hi")
    core = lax.axis_index("core")
    y = lax.axis_index("y")
    me = 2 * y + half
    for k, block in enumerate((own0, own1, own2, own3)):
        s = 2 * lax.rem(y + 4 - k, 4) + half
        weights[s] = block[:, :256]
        pre_emb[s] = (block[:, 256:320].astype(F32) + block[:, 320:384].astype(F32)).T
    for k in range(count // 2):
        s = 2 * k + 1 - half
        weights[s, :inner] = other[k, 0, :, :256]
        weights[s, inner:] = other[k, 1, :, :256]
        mine = other[k, core, :, 256:384].astype(F32).T
        pre_emb[s] = jnp.concatenate([mine[:64], mine[64:]], axis=1)
    for s in range(count):
        turned[s] = weights[s].T

    eu = emb_basis[...]
    sq = norm[...]
    c = jnp.zeros(eu.shape, BF16)
    c_kept[0] = c
    invs = []
    for s in range(count):
        cf = c.astype(F32)
        pre = pre_emb[s]
        total = sq
        if s:
            pre = pre + dot(weights[s, :inner], c)
            total = total + jnp.sum(cf * (2.0 * eu + cf), axis=0, keepdims=True)
        inv = lax.rsqrt(jnp.maximum(total, 0.0) * (1.0 / width) + EPS)
        invs.append(inv)
        pre = pre * inv
        sig = 1.0 / (1.0 + jnp.exp(-pre))
        act = (pre * sig).astype(BF16)
        pre_kept[s] = pre
        slope_kept[s] = sig * (1.0 + pre * (1.0 - sig))
        a_kept[s] = act
        c = (cf + dot(turned[s, :, inner:], act)).astype(BF16)
        c_kept[s + 1] = c
    coefs[...] = c_kept[me + 1].T
    coefs_copy = pltpu.make_async_copy(coefs, coefs_hbm, coefs_sem)
    coefs_copy.start()

    g = cotangent[...].T
    for s in reversed(range(count)):
        g_kept[s] = g
        inv = invs[s]
        gp = (dot(weights[s, inner:], g) * slope_kept[s]).astype(BF16)
        gpf = gp.astype(F32)
        p_kept[s] = (gpf * inv).astype(BF16)
        if s:
            mean = jnp.sum(gpf * pre_kept[s], axis=0, keepdims=True) * (1.0 / width)
            back = dot(turned[s, :, :inner], gp)
            hid = eu + c_kept[s].astype(F32)
            g = (g.astype(F32) + inv * back - (inv * inv * mean) * hid).astype(BF16)

    p_t = p_kept[me]
    cp = dot(p_t, c_kept[me], NT).astype(BF16)
    s2 = dot(a_kept[me], g_kept[me], NT).astype(BF16)
    low = lax.broadcasted_iota(jnp.int32, (inner, 128), 1) < 64
    for x in range(4):
        spans = [slice((zl * 4 + x) * 128, (zl * 4 + x) * 128 + 128) for zl in range(8)]
        tiles = jnp.concatenate([emb[:, at] for at in spans], axis=1)
        rows = jnp.concatenate([basis[at, :] for at in spans], axis=0)
        scale = jnp.concatenate([gain[:, at] for at in spans], axis=1)
        grad = (dot(p_t, tiles) + dot(cp, rows, NT)) * scale
        for q in range(4):
            first = grad[:, 256 * q : 256 * q + 128]
            second = grad[:, 256 * q + 128 : 256 * q + 256]
            lanes = slice(q * 128, q * 128 + 128)
            slots[2 * x, :, lanes] = jnp.where(low, first, pltpu.roll(second, 64, 1)).astype(BF16)
            slots[2 * x + 1, :, lanes] = jnp.where(low, pltpu.roll(first, 64, 1), second).astype(BF16)
        for j in (2 * x, 2 * x + 1):
            slots[j, :, 512:768] = s2
    coefs_copy.wait()


def chain(own, other, norm, emb_basis, cotangent, embeds, basis, gain):
    count = 2 * len(own)
    rows, rank = cotangent.shape
    inner = 64
    hbm = pl.BlockSpec(memory_space=pltpu.HBM)
    vmem = pl.BlockSpec(memory_space=pltpu.VMEM)
    return pl.pallas_call(
        chain_kernel,
        in_specs=[vmem] * 11,
        out_specs=[hbm, vmem],
        out_shape=[
            pltpu.HBM((rows, rank), BF16),
            jax.ShapeDtypeStruct((8, inner, 768), BF16),
        ],
        scratch_shapes=[
            pltpu.VMEM((count, 2 * inner, rank), BF16),
            pltpu.VMEM((count, rank, 2 * inner), BF16),
            pltpu.VMEM((count, inner, rows), F32),
            pltpu.VMEM((count + 1, rank, rows), BF16),
            pltpu.VMEM((count, rank, rows), BF16),
            pltpu.VMEM((count, inner, rows), BF16),
            pltpu.VMEM((count, inner, rows), BF16),
            pltpu.VMEM((count, inner, rows), F32),
            pltpu.VMEM((count, inner, rows), F32),
            pltpu.VMEM((rows, rank), BF16),
            pltpu.SemaphoreType.DMA,
        ],
        compiler_params=pltpu.CompilerParams(vmem_limit_bytes=32 * 1024 * 1024),
        name="chain",
    )(*own, other, norm, emb_basis, cotangent, embeds, basis, gain)


def middle_kernel(got, basis, out):
    total = got[0].astype(F32)
    for j in range(1, got.shape[0]):
        total = total + got[j].astype(F32)
    lane = 2 * lax.axis_index("x") + lax.axis_index("core")
    rows = basis[:, lane].reshape(512, 256)
    w2 = dot(total[:, 512:].astype(BF16), rows, NT)
    both = jnp.concatenate([total[:, :512], w2], axis=0)
    out[...] = both.T.astype(BF16).reshape(out.shape)


def middle(got, basis):
    return pl.pallas_call(
        middle_kernel,
        in_specs=[pl.BlockSpec(memory_space=pltpu.VMEM)] * 2,
        out_specs=pl.BlockSpec(memory_space=pltpu.VMEM),
        out_shape=jax.ShapeDtypeStruct((8, 64, 128), BF16),
        compiler_params=pltpu.CompilerParams(vmem_limit_bytes=32 * 1024 * 1024),
        name="middle",
    )(got, basis.reshape(8, 8, 64, 256))


def final_kernel(got, out):
    total = got[0].astype(F32)
    for j in range(1, got.shape[0]):
        total = total + got[j].astype(F32)
    out[...] = total


def final(got):
    return pl.pallas_call(
        final_kernel,
        out_shape=jax.ShapeDtypeStruct(got.shape[1:], F32),
        compiler_params=pltpu.CompilerParams(vmem_limit_bytes=4 * 1024 * 1024),
        name="final",
    )(got)


def local(embeds, shared_basis, down_proj, up_proj, norm_gain, coef_grad):
    block, part, emb_basis, norm = project(
        embeds, shared_basis, down_proj[0].T, up_proj[0].T, norm_gain
    )
    crossed = lax.ppermute(part, "z_hi", [(0, 1), (1, 0)])
    own = [block] + [lax.ppermute(block, "y", [(i, (i + k) % 4) for i in range(4)]) for k in (1, 2, 3)]
    other = lax.all_gather(crossed, ("y", "core"), tiled=False).reshape((4, 2) + part.shape)
    coefs, slots = chain(own, other, norm, emb_basis, coef_grad, embeds, shared_basis, norm_gain)
    got = lax.all_to_all(slots, ("x", "core"), 0, 0, tiled=True)
    summed = middle(got, shared_basis)
    got = lax.all_to_all(summed, "z_lo", 0, 0, tiled=True)
    return coefs[None], final(got)[None]


def solution(mesh):
    fine = Mesh(mesh.devices.reshape(SIZES), AXES)
    placed = (
        P(REPLICA, None),
        P(),
        P(SECTION, None, None),
        P(SECTION, None, None),
        P(SECTION, None),
        P(REPLICA, None),
    )
    return jax.shard_map(
        local,
        mesh=fine,
        in_specs=placed,
        out_specs=(P(SECTION, REPLICA, None), P(SECTION, REPLICA, None)),
        check_vma=False,
    )
```

```python
import functools

import jax
import jax.numpy as jnp
from jax import lax
from jax.experimental import pallas as pl
from jax.experimental.pallas import tpu as pltpu
from jax.sharding import Mesh, PartitionSpec as P

F32 = jnp.float32
BF16 = jnp.bfloat16
EPS = 1e-05
SECTION = ("y", "z_hi")
REPLICA = ("z_far", "z_near", "x", "core")
AXES = SECTION + REPLICA
SIZES = (4, 2, 4, 2, 4, 2)

NN = (((1,), (0,)), ((), ()))
NT = (((1,), (1,)), ((), ()))
TN = (((0,), (0,)), ((), ()))


def dot(a, b, dims=NN):
    return lax.dot_general(a, b, dims, preferred_element_type=F32)


def project_kernel(
    chunk, emb_hbm, basis_hbm, down_hbm, up_hbm, gain_hbm,
    block, part, emb_basis, norm, emb, basis, down, up, gain, sems,
):
    rows, width = emb.shape
    steps = width // chunk
    gain_copy = pltpu.make_async_copy(gain_hbm, gain, sems.at[4, 0])
    gain_copy.start()
    copies = []
    for i in range(steps):
        at = slice(i * chunk, (i + 1) * chunk)
        group = [
            pltpu.make_async_copy(down_hbm.at[:, at], down.at[:, at], sems.at[0, i]),
            pltpu.make_async_copy(up_hbm.at[:, at], up.at[:, at], sems.at[1, i]),
            pltpu.make_async_copy(emb_hbm.at[:, at], emb.at[:, at], sems.at[2, i]),
            pltpu.make_async_copy(basis_hbm.at[at, :], basis.at[at, :], sems.at[3, i]),
        ]
        for copy in group:
            copy.start()
        copies.append(group)
    gain_copy.wait()
    acc = jnp.zeros((rows + 128, basis.shape[1]), F32)
    acc_pre = jnp.zeros((rows, 64), F32)
    square = jnp.zeros((rows, 128), F32)
    for i in range(steps):
        at = slice(i * chunk, (i + 1) * chunk)
        for copy in copies[i]:
            copy.wait()
        e = emb[:, at]
        scaled = (down[:, at].astype(F32) * gain[:, at]).astype(BF16)
        stacked = jnp.concatenate([e, scaled, up[:, at]], axis=0)
        acc = acc + dot(stacked, basis[at, :])
        acc_pre = acc_pre + dot(e, scaled, NT)
        ef = e.astype(F32)
        sq = ef * ef
        for k in range(0, chunk, 128):
            square = square + sq[:, k : k + 128]
    emb_basis[...] = acc[:rows, :].T
    high = acc_pre.astype(BF16)
    block[:, :256] = acc[rows:, :].astype(BF16)
    block[:, 256:320] = high
    block[:, 320:384] = (acc_pre - high.astype(F32)).astype(BF16)
    first = lax.axis_index("core") == 0
    weights = jnp.where(first, acc[rows : rows + 64, :], acc[rows + 64 :, :])
    part[:, :256] = weights.astype(BF16)
    part[:, 256:320] = high[:64]
    part[:, 320:384] = high[64:]
    norm[...] = jnp.sum(square.T, axis=0, keepdims=True)


def project(embeds, basis, down_t, up_t, gain):
    rows, width = embeds.shape
    rank = basis.shape[1]
    inner = down_t.shape[0]
    chunk = 512
    hbm = pl.BlockSpec(memory_space=pltpu.HBM)
    vmem = pl.BlockSpec(memory_space=pltpu.VMEM)
    args = [pltpu.with_memory_space_constraint(a, pltpu.HBM) for a in (embeds, basis, down_t, up_t, gain)]
    return pl.pallas_call(
        functools.partial(project_kernel, chunk),
        in_specs=[hbm] * 5,
        out_specs=[vmem] * 4,
        out_shape=[
            jax.ShapeDtypeStruct((2 * inner, rank + 2 * inner), BF16),
            jax.ShapeDtypeStruct((inner, rank + 2 * inner), BF16),
            jax.ShapeDtypeStruct((rank, rows), F32),
            jax.ShapeDtypeStruct((1, rows), F32),
        ],
        scratch_shapes=[
            pltpu.VMEM((rows, width), BF16),
            pltpu.VMEM((width, rank), BF16),
            pltpu.VMEM((inner, width), BF16),
            pltpu.VMEM((inner, width), BF16),
            pltpu.VMEM((1, width), F32),
            pltpu.SemaphoreType.DMA((5, width // chunk)),
        ],
        compiler_params=pltpu.CompilerParams(vmem_limit_bytes=24 * 1024 * 1024),
        name="project",
    )(*args)


def chain_kernel(
    own0, own1, own2, own3, other, norm, emb_basis, cotangent, emb, basis, gain,
    coefs_hbm, kept, sent,
    weights, turned, pre_emb, c_kept, g_kept, p_kept, a_kept, pre_kept, slope_kept, coefs, coefs_sem,
):
    count = weights.shape[0]
    width = emb.shape[1]
    inner = 64
    half = lax.axis_index("z_hi")
    core = lax.axis_index("core")
    y = lax.axis_index("y")
    me = 2 * y + half
    for k, block in enumerate((own0, own1, own2, own3)):
        s = 2 * lax.rem(y + 4 - k, 4) + half
        weights[s] = block[:, :256]
        pre_emb[s] = (block[:, 256:320].astype(F32) + block[:, 320:384].astype(F32)).T
    for k in range(count // 2):
        s = 2 * k + 1 - half
        weights[s, :inner] = other[k, 0, :, :256]
        weights[s, inner:] = other[k, 1, :, :256]
        mine = other[k, core, :, 256:384].astype(F32).T
        pre_emb[s] = jnp.concatenate([mine[:64], mine[64:]], axis=1)
    for s in range(count):
        turned[s] = weights[s].T

    eu = emb_basis[...]
    sq = norm[...]
    c = jnp.zeros(eu.shape, BF16)
    c_kept[0] = c
    invs = []
    for s in range(count):
        cf = c.astype(F32)
        pre = pre_emb[s]
        total = sq
        if s:
            pre = pre + dot(weights[s, :inner], c)
            total = total + jnp.sum(cf * (2.0 * eu + cf), axis=0, keepdims=True)
        inv = lax.rsqrt(jnp.maximum(total, 0.0) * (1.0 / width) + EPS)
        invs.append(inv)
        pre = pre * inv
        sig = 1.0 / (1.0 + jnp.exp(-pre))
        act = (pre * sig).astype(BF16)
        pre_kept[s] = pre
        slope_kept[s] = sig * (1.0 + pre * (1.0 - sig))
        a_kept[s] = act
        c = (cf + dot(turned[s, :, inner:], act)).astype(BF16)
        c_kept[s + 1] = c
    coefs[...] = c_kept[me + 1].T
    coefs_copy = pltpu.make_async_copy(coefs, coefs_hbm, coefs_sem)
    coefs_copy.start()

    g = cotangent[...].T
    for s in reversed(range(count)):
        g_kept[s] = g
        inv = invs[s]
        gp = (dot(weights[s, inner:], g) * slope_kept[s]).astype(BF16)
        gpf = gp.astype(F32)
        p_kept[s] = (gpf * inv).astype(BF16)
        if s:
            mean = jnp.sum(gpf * pre_kept[s], axis=0, keepdims=True) * (1.0 / width)
            back = dot(turned[s, :, :inner], gp)
            hid = eu + c_kept[s].astype(F32)
            g = (g.astype(F32) + inv * back - (inv * inv * mean) * hid).astype(BF16)

    p_t = p_kept[me]
    cp = dot(p_t, c_kept[me], NT).astype(BF16)
    s2 = dot(a_kept[me], g_kept[me], NT)
    kept[8] = s2
    sent[8] = s2.astype(BF16)
    low = lax.broadcasted_iota(jnp.int32, (inner, 128), 1) < 64
    first_core = core == 0
    for j in range(8):
        spans = [slice(far * 1024 + j * 128, far * 1024 + j * 128 + 128) for far in range(4)]
        tiles = jnp.concatenate([emb[:, at] for at in spans], axis=1)
        rows = jnp.concatenate([basis[at, :] for at in spans], axis=0)
        scale = jnp.concatenate([gain[:, at] for at in spans], axis=1)
        grad = (dot(p_t, tiles) + dot(cp, rows, NT)) * scale
        for q in range(2):
            one = grad[:, 256 * q : 256 * q + 128]
            two = grad[:, 256 * q + 128 : 256 * q + 256]
            lanes = slice(q * 128, q * 128 + 128)
            zero = jnp.where(low, one, pltpu.roll(two, 64, 1))
            other_half = jnp.where(low, pltpu.roll(one, 64, 1), two)
            kept[j, :, lanes] = jnp.where(first_core, zero, other_half)
            sent[j, :, lanes] = jnp.where(first_core, other_half, zero).astype(BF16)
    coefs_copy.wait()


def chain(own, other, norm, emb_basis, cotangent, embeds, basis, gain):
    count = 2 * len(own)
    rows, rank = cotangent.shape
    inner = 64
    hbm = pl.BlockSpec(memory_space=pltpu.HBM)
    vmem = pl.BlockSpec(memory_space=pltpu.VMEM)
    return pl.pallas_call(
        chain_kernel,
        in_specs=[vmem] * 11,
        out_specs=[hbm, vmem, vmem],
        out_shape=[
            pltpu.HBM((rows, rank), BF16),
            jax.ShapeDtypeStruct((9, inner, 256), F32),
            jax.ShapeDtypeStruct((9, inner, 256), BF16),
        ],
        scratch_shapes=[
            pltpu.VMEM((count, 2 * inner, rank), BF16),
            pltpu.VMEM((count, rank, 2 * inner), BF16),
            pltpu.VMEM((count, inner, rows), F32),
            pltpu.VMEM((count + 1, rank, rows), BF16),
            pltpu.VMEM((count, rank, rows), BF16),
            pltpu.VMEM((count, inner, rows), BF16),
            pltpu.VMEM((count, inner, rows), BF16),
            pltpu.VMEM((count, inner, rows), F32),
            pltpu.VMEM((count, inner, rows), F32),
            pltpu.VMEM((rows, rank), BF16),
            pltpu.SemaphoreType.DMA,
        ],
        compiler_params=pltpu.CompilerParams(vmem_limit_bytes=32 * 1024 * 1024),
        name="chain",
    )(*own, other, norm, emb_basis, cotangent, embeds, basis, gain)


def merge_kernel(kept, got, out):
    weights = (kept[8] + got[8].astype(F32)).astype(BF16)
    for j in range(8):
        out[j, :, :256] = (kept[j] + got[j].astype(F32)).astype(BF16)
        out[j, :, 256:] = weights


def merge(kept, got):
    return pl.pallas_call(
        merge_kernel,
        out_shape=jax.ShapeDtypeStruct((8, 64, 512), BF16),
        compiler_params=pltpu.CompilerParams(vmem_limit_bytes=8 * 1024 * 1024),
        name="merge",
    )(kept, got)


def middle_kernel(got, basis, out):
    total = got[0].astype(F32)
    for j in range(1, got.shape[0]):
        total = total + got[j].astype(F32)
    lane = 4 * lax.axis_index("z_near") + lax.axis_index("x")
    rows = basis[:, lane, lax.axis_index("core")].reshape(256, 256)
    w2 = dot(total[:, 256:].astype(BF16), rows, NT)
    both = jnp.concatenate([total[:, :256], w2], axis=0)
    out[...] = both.T.astype(BF16).reshape(out.shape)


def middle(got, basis):
    return pl.pallas_call(
        middle_kernel,
        in_specs=[pl.BlockSpec(memory_space=pltpu.VMEM)] * 2,
        out_specs=pl.BlockSpec(memory_space=pltpu.VMEM),
        out_shape=jax.ShapeDtypeStruct((4, 64, 128), BF16),
        compiler_params=pltpu.CompilerParams(vmem_limit_bytes=16 * 1024 * 1024),
        name="middle",
    )(got, basis.reshape(4, 8, 2, 64, 256))


def final_kernel(got, out):
    total = got[0].astype(F32)
    for j in range(1, got.shape[0]):
        total = total + got[j].astype(F32)
    out[...] = total


def final(got):
    return pl.pallas_call(
        final_kernel,
        out_shape=jax.ShapeDtypeStruct(got.shape[1:], F32),
        compiler_params=pltpu.CompilerParams(vmem_limit_bytes=4 * 1024 * 1024),
        name="final",
    )(got)


def local(embeds, shared_basis, down_proj, up_proj, norm_gain, coef_grad):
    block, part, emb_basis, norm = project(
        embeds, shared_basis, down_proj[0].T, up_proj[0].T, norm_gain
    )
    crossed = lax.ppermute(part, "z_hi", [(0, 1), (1, 0)])
    own = [block] + [lax.ppermute(block, "y", [(i, (i + k) % 4) for i in range(4)]) for k in (1, 2, 3)]
    other = lax.all_gather(crossed, ("y", "core"), tiled=False)
    other = other.reshape((4, 2) + part.shape)
    coefs, kept, sent = chain(own, other, norm, emb_basis, coef_grad, embeds, shared_basis, norm_gain)
    got = lax.ppermute(sent, "core", [(0, 1), (1, 0)])
    got = lax.all_to_all(merge(kept, got), ("z_near", "x"), 0, 0, tiled=True)
    got = lax.all_to_all(middle(got, shared_basis), "z_far", 0, 0, tiled=True)
    return coefs[None], final(got)[None]


def solution(mesh):
    fine = Mesh(mesh.devices.reshape(SIZES), AXES)
    placed = (
        P(REPLICA, None),
        P(),
        P(SECTION, None, None),
        P(SECTION, None, None),
        P(SECTION, None),
        P(REPLICA, None),
    )
    return jax.shard_map(
        local,
        mesh=fine,
        in_specs=placed,
        out_specs=(P(SECTION, REPLICA, None), P(SECTION, REPLICA, None)),
        check_vma=False,
    )
```

```python
import functools

import jax
import jax.numpy as jnp
from jax import lax
from jax.experimental import pallas as pl
from jax.experimental.pallas import tpu as pltpu
from jax.sharding import Mesh, PartitionSpec as P

F32 = jnp.float32
BF16 = jnp.bfloat16
EPS = 1e-05
SECTION = ("y", "z_hi")
REPLICA = ("z_far", "z_near", "x", "core")
AXES = SECTION + REPLICA
SIZES = (4, 2, 4, 2, 4, 2)

NN = (((1,), (0,)), ((), ()))
NT = (((1,), (1,)), ((), ()))
TN = (((0,), (0,)), ((), ()))


def dot(a, b, dims=NN):
    return lax.dot_general(a, b, dims, preferred_element_type=F32)


def project_kernel(
    chunk, emb_hbm, basis_hbm, down_hbm, up_hbm, gain_hbm,
    part, emb_basis, norm, emb, basis, down, up, gain, sems,
):
    rows, width = emb.shape
    steps = width // chunk
    gain_copy = pltpu.make_async_copy(gain_hbm, gain, sems.at[4, 0])
    gain_copy.start()
    copies = []
    for i in range(steps):
        at = slice(i * chunk, (i + 1) * chunk)
        group = [
            pltpu.make_async_copy(down_hbm.at[:, at], down.at[:, at], sems.at[0, i]),
            pltpu.make_async_copy(up_hbm.at[:, at], up.at[:, at], sems.at[1, i]),
            pltpu.make_async_copy(emb_hbm.at[:, at], emb.at[:, at], sems.at[2, i]),
            pltpu.make_async_copy(basis_hbm.at[at, :], basis.at[at, :], sems.at[3, i]),
        ]
        for copy in group:
            copy.start()
        copies.append(group)
    gain_copy.wait()
    acc = jnp.zeros((rows + 128, basis.shape[1]), F32)
    acc_pre = jnp.zeros((rows, 64), F32)
    square = jnp.zeros((rows, 128), F32)
    for i in range(steps):
        at = slice(i * chunk, (i + 1) * chunk)
        for copy in copies[i]:
            copy.wait()
        e = emb[:, at]
        scaled = (down[:, at].astype(F32) * gain[:, at]).astype(BF16)
        stacked = jnp.concatenate([e, scaled, up[:, at]], axis=0)
        acc = acc + dot(stacked, basis[at, :])
        acc_pre = acc_pre + dot(e, scaled, NT)
        ef = e.astype(F32)
        sq = ef * ef
        for k in range(0, chunk, 128):
            square = square + sq[:, k : k + 128]
    emb_basis[...] = acc[:rows, :].T
    first = lax.axis_index("core") == 0
    weights = jnp.where(first, acc[rows : rows + 64, :], acc[rows + 64 :, :])
    part[:, :256] = weights.astype(BF16)
    part[:, 256:320] = acc_pre[:64].astype(BF16)
    part[:, 320:384] = acc_pre[64:].astype(BF16)
    norm[...] = jnp.sum(square.T, axis=0, keepdims=True)


def project(embeds, basis, down_t, up_t, gain):
    rows, width = embeds.shape
    rank = basis.shape[1]
    inner = down_t.shape[0]
    chunk = 1024
    hbm = pl.BlockSpec(memory_space=pltpu.HBM)
    vmem = pl.BlockSpec(memory_space=pltpu.VMEM)
    args = [pltpu.with_memory_space_constraint(a, pltpu.HBM) for a in (embeds, basis, down_t, up_t, gain)]
    return pl.pallas_call(
        functools.partial(project_kernel, chunk),
        in_specs=[hbm] * 5,
        out_specs=[vmem] * 3,
        out_shape=[
            jax.ShapeDtypeStruct((inner, rank + 2 * inner), BF16),
            jax.ShapeDtypeStruct((rank, rows), F32),
            jax.ShapeDtypeStruct((1, rows), F32),
        ],
        scratch_shapes=[
            pltpu.VMEM((rows, width), BF16),
            pltpu.VMEM((width, rank), BF16),
            pltpu.VMEM((inner, width), BF16),
            pltpu.VMEM((inner, width), BF16),
            pltpu.VMEM((1, width), F32),
            pltpu.SemaphoreType.DMA((5, width // chunk)),
        ],
        compiler_params=pltpu.CompilerParams(vmem_limit_bytes=24 * 1024 * 1024),
        name="project",
    )(*args)


def join_kernel(part, crossed, out):
    out[0] = part[...]
    out[1] = crossed[...]


def join(part, crossed):
    return pl.pallas_call(
        join_kernel,
        out_shape=jax.ShapeDtypeStruct((2,) + part.shape, part.dtype),
        compiler_params=pltpu.CompilerParams(vmem_limit_bytes=4 * 1024 * 1024),
        name="join",
    )(part, crossed)


def chain_kernel(
    every, norm, emb_basis, cotangent, emb, basis, gain,
    coefs_hbm, kept, sent,
    weights, turned, pre_emb, c_kept, g_kept, p_kept, a_kept, pre_kept, slope_kept, coefs, coefs_sem,
):
    count = weights.shape[0]
    width = emb.shape[1]
    inner = 64
    half = lax.axis_index("z_hi")
    core = lax.axis_index("core")
    y = lax.axis_index("y")
    me = 2 * y + half
    for k in range(count // 2):
        for side in range(2):
            s = 2 * k + (1 - half if side else half)
            weights[s, :inner] = every[k, 0, side, :, :256]
            weights[s, inner:] = every[k, 1, side, :, :256]
            mine = every[k, core, side, :, 256:384].astype(F32).T
            pre_emb[s] = jnp.concatenate([mine[:64], mine[64:]], axis=1)
    for s in range(count):
        turned[s] = weights[s].T

    eu = emb_basis[...]
    sq = norm[...]
    c = jnp.zeros(eu.shape, BF16)
    c_kept[0] = c
    invs = []
    for s in range(count):
        cf = c.astype(F32)
        pre = pre_emb[s]
        total = sq
        if s:
            pre = pre + dot(weights[s, :inner], c)
            total = total + jnp.sum(cf * (2.0 * eu + cf), axis=0, keepdims=True)
        inv = lax.rsqrt(jnp.maximum(total, 0.0) * (1.0 / width) + EPS)
        invs.append(inv)
        pre = pre * inv
        sig = 1.0 / (1.0 + jnp.exp(-pre))
        act = (pre * sig).astype(BF16)
        pre_kept[s] = pre
        slope_kept[s] = sig * (1.0 + pre * (1.0 - sig))
        a_kept[s] = act
        c = (cf + dot(turned[s, :, inner:], act)).astype(BF16)
        c_kept[s + 1] = c
    coefs[...] = c_kept[me + 1].T
    coefs_copy = pltpu.make_async_copy(coefs, coefs_hbm, coefs_sem)
    coefs_copy.start()

    g = cotangent[...].T
    for s in reversed(range(count)):
        g_kept[s] = g
        inv = invs[s]
        gp = (dot(weights[s, inner:], g) * slope_kept[s]).astype(BF16)
        gpf = gp.astype(F32)
        p_kept[s] = (gpf * inv).astype(BF16)
        if s:
            mean = jnp.sum(gpf * pre_kept[s], axis=0, keepdims=True) * (1.0 / width)
            back = dot(turned[s, :, :inner], gp)
            hid = eu + c_kept[s].astype(F32)
            g = (g.astype(F32) + inv * back - (inv * inv * mean) * hid).astype(BF16)

    p_t = p_kept[me]
    cp = dot(p_t, c_kept[me], NT).astype(BF16)
    s2 = dot(a_kept[me], g_kept[me], NT)
    kept[8] = s2
    sent[8] = s2.astype(BF16)
    low = lax.broadcasted_iota(jnp.int32, (inner, 128), 1) < 64
    first_core = core == 0
    for j in range(8):
        spans = [slice(far * 1024 + j * 128, far * 1024 + j * 128 + 128) for far in range(4)]
        tiles = jnp.concatenate([emb[:, at] for at in spans], axis=1)
        rows = jnp.concatenate([basis[at, :] for at in spans], axis=0)
        scale = jnp.concatenate([gain[:, at] for at in spans], axis=1)
        grad = (dot(p_t, tiles) + dot(cp, rows, NT)) * scale
        for q in range(2):
            one = grad[:, 256 * q : 256 * q + 128]
            two = grad[:, 256 * q + 128 : 256 * q + 256]
            lanes = slice(q * 128, q * 128 + 128)
            zero = jnp.where(low, one, pltpu.roll(two, 64, 1))
            other_half = jnp.where(low, pltpu.roll(one, 64, 1), two)
            kept[j, :, lanes] = jnp.where(first_core, zero, other_half)
            sent[j, :, lanes] = jnp.where(first_core, other_half, zero).astype(BF16)
    coefs_copy.wait()


def chain(every, norm, emb_basis, cotangent, embeds, basis, gain):
    count = 2 * every.shape[0]
    rows, rank = cotangent.shape
    inner = 64
    hbm = pl.BlockSpec(memory_space=pltpu.HBM)
    vmem = pl.BlockSpec(memory_space=pltpu.VMEM)
    return pl.pallas_call(
        chain_kernel,
        in_specs=[vmem] * 7,
        out_specs=[hbm, vmem, vmem],
        out_shape=[
            pltpu.HBM((rows, rank), BF16),
            jax.ShapeDtypeStruct((9, inner, 256), F32),
            jax.ShapeDtypeStruct((9, inner, 256), BF16),
        ],
        scratch_shapes=[
            pltpu.VMEM((count, 2 * inner, rank), BF16),
            pltpu.VMEM((count, rank, 2 * inner), BF16),
            pltpu.VMEM((count, inner, rows), F32),
            pltpu.VMEM((count + 1, rank, rows), BF16),
            pltpu.VMEM((count, rank, rows), BF16),
            pltpu.VMEM((count, inner, rows), BF16),
            pltpu.VMEM((count, inner, rows), BF16),
            pltpu.VMEM((count, inner, rows), F32),
            pltpu.VMEM((count, inner, rows), F32),
            pltpu.VMEM((rows, rank), BF16),
            pltpu.SemaphoreType.DMA,
        ],
        compiler_params=pltpu.CompilerParams(vmem_limit_bytes=32 * 1024 * 1024),
        name="chain",
    )(every, norm, emb_basis, cotangent, embeds, basis, gain)


def merge_kernel(kept, got, out):
    weights = (kept[8] + got[8].astype(F32)).astype(BF16)
    for j in range(8):
        out[j, :, :256] = (kept[j] + got[j].astype(F32)).astype(BF16)
        out[j, :, 256:] = weights


def merge(kept, got):
    return pl.pallas_call(
        merge_kernel,
        out_shape=jax.ShapeDtypeStruct((8, 64, 512), BF16),
        compiler_params=pltpu.CompilerParams(vmem_limit_bytes=8 * 1024 * 1024),
        name="merge",
    )(kept, got)


def middle_kernel(got, basis, out):
    total = got[0].astype(F32)
    for j in range(1, got.shape[0]):
        total = total + got[j].astype(F32)
    lane = 4 * lax.axis_index("z_near") + lax.axis_index("x")
    rows = basis[:, lane, lax.axis_index("core")].reshape(256, 256)
    w2 = dot(total[:, 256:].astype(BF16), rows, NT)
    both = jnp.concatenate([total[:, :256], w2], axis=0)
    out[...] = both.T.astype(BF16).reshape(out.shape)


def middle(got, basis):
    return pl.pallas_call(
        middle_kernel,
        in_specs=[pl.BlockSpec(memory_space=pltpu.VMEM)] * 2,
        out_specs=pl.BlockSpec(memory_space=pltpu.VMEM),
        out_shape=jax.ShapeDtypeStruct((4, 64, 128), BF16),
        compiler_params=pltpu.CompilerParams(vmem_limit_bytes=16 * 1024 * 1024),
        name="middle",
    )(got, basis.reshape(4, 8, 2, 64, 256))


def final_kernel(got, out):
    total = got[0].astype(F32)
    for j in range(1, got.shape[0]):
        total = total + got[j].astype(F32)
    out[...] = total


def final(got):
    return pl.pallas_call(
        final_kernel,
        out_shape=jax.ShapeDtypeStruct(got.shape[1:], F32),
        compiler_params=pltpu.CompilerParams(vmem_limit_bytes=4 * 1024 * 1024),
        name="final",
    )(got)


def local(embeds, shared_basis, down_proj, up_proj, norm_gain, coef_grad):
    part, emb_basis, norm = project(
        embeds, shared_basis, down_proj[0].T, up_proj[0].T, norm_gain
    )
    crossed = lax.ppermute(part, "z_hi", [(0, 1), (1, 0)])
    every = lax.all_gather(join(part, crossed), ("y", "core"), tiled=False)
    every = every.reshape((4, 2, 2) + part.shape)
    coefs, kept, sent = chain(every, norm, emb_basis, coef_grad, embeds, shared_basis, norm_gain)
    got = lax.ppermute(sent, "core", [(0, 1), (1, 0)])
    got = lax.all_to_all(merge(kept, got), ("z_near", "x"), 0, 0, tiled=True)
    got = lax.all_to_all(middle(got, shared_basis), "z_far", 0, 0, tiled=True)
    return coefs[None], final(got)[None]


def solution(mesh):
    fine = Mesh(mesh.devices.reshape(SIZES), AXES)
    placed = (
        P(REPLICA, None),
        P(),
        P(SECTION, None, None),
        P(SECTION, None, None),
        P(SECTION, None),
        P(REPLICA, None),
    )
    return jax.shard_map(
        local,
        mesh=fine,
        in_specs=placed,
        out_specs=(P(SECTION, REPLICA, None), P(SECTION, REPLICA, None)),
        check_vma=False,
    )
```

```python
import functools

import jax
import jax.numpy as jnp
from jax import lax
from jax.experimental import pallas as pl
from jax.experimental.pallas import tpu as pltpu
from jax.sharding import Mesh, PartitionSpec as P

F32 = jnp.float32
BF16 = jnp.bfloat16
EPS = 1e-05
SECTION = ("y", "z_hi")
REPLICA = ("z_far", "z_near", "x", "core")
AXES = SECTION + REPLICA
SIZES = (4, 2, 4, 2, 4, 2)

NN = (((1,), (0,)), ((), ()))
NT = (((1,), (1,)), ((), ()))
TN = (((0,), (0,)), ((), ()))


def dot(a, b, dims=NN):
    return lax.dot_general(a, b, dims, preferred_element_type=F32)


def project_kernel(
    chunk, emb_hbm, basis_hbm, down_hbm, up_hbm, gain_hbm,
    part, emb, basis, down, up, gain, sems,
):
    rows, width = emb.shape
    inner = down.shape[0]
    steps = width // chunk
    gain_copy = pltpu.make_async_copy(gain_hbm, gain, sems.at[4, 0])
    gain_copy.start()
    copies = []
    for i in range(steps):
        at = slice(i * chunk, (i + 1) * chunk)
        group = [
            pltpu.make_async_copy(down_hbm.at[:, at], down.at[:, at], sems.at[0, i]),
            pltpu.make_async_copy(up_hbm.at[:, at], up.at[:, at], sems.at[1, i]),
            pltpu.make_async_copy(emb_hbm.at[:, at], emb.at[:, at], sems.at[2, i]),
            pltpu.make_async_copy(basis_hbm.at[at, :], basis.at[at, :], sems.at[3, i]),
        ]
        for copy in group:
            copy.start()
        copies.append(group)
    gain_copy.wait()
    acc = jnp.zeros((2 * inner, basis.shape[1]), F32)
    pre = jnp.zeros((inner, rows), F32)
    for i in range(steps):
        at = slice(i * chunk, (i + 1) * chunk)
        for copy in copies[i]:
            copy.wait()
        scaled = (down[:, at].astype(F32) * gain[:, at]).astype(BF16)
        acc = acc + dot(jnp.concatenate([scaled, up[:, at]], axis=0), basis[at, :])
        pre = pre + dot(scaled, emb[:, at], NT)
    first = lax.axis_index("core") == 0
    part[:, :256] = jnp.where(first, acc[:inner], acc[inner:]).astype(BF16)
    part[:, 256:] = pre.astype(BF16)


def project(embeds, basis, down_t, up_t, gain):
    rows, width = embeds.shape
    rank = basis.shape[1]
    inner = down_t.shape[0]
    chunk = 1024
    args = [pltpu.with_memory_space_constraint(a, pltpu.HBM) for a in (embeds, basis, down_t, up_t, gain)]
    return pl.pallas_call(
        functools.partial(project_kernel, chunk),
        in_specs=[pl.BlockSpec(memory_space=pltpu.HBM)] * 5,
        out_specs=pl.BlockSpec(memory_space=pltpu.VMEM),
        out_shape=jax.ShapeDtypeStruct((inner, rank + rows), BF16),
        scratch_shapes=[
            pltpu.VMEM((rows, width), BF16),
            pltpu.VMEM((width, rank), BF16),
            pltpu.VMEM((inner, width), BF16),
            pltpu.VMEM((inner, width), BF16),
            pltpu.VMEM((1, width), F32),
            pltpu.SemaphoreType.DMA((5, width // chunk)),
        ],
        compiler_params=pltpu.CompilerParams(vmem_limit_bytes=24 * 1024 * 1024),
        name="project",
    )(*args)


def embed_kernel(emb, basis, emb_basis, norm):
    rows, width = emb.shape
    chunk = 1024
    acc = jnp.zeros((rows, basis.shape[1]), F32)
    square = jnp.zeros((rows, 128), F32)
    for at in range(0, width, chunk):
        e = emb[:, at : at + chunk]
        acc = acc + dot(e, basis[at : at + chunk, :])
        ef = e.astype(F32)
        sq = ef * ef
        for k in range(0, chunk, 128):
            square = square + sq[:, k : k + 128]
    emb_basis[...] = acc.T
    norm[...] = jnp.sum(square.T, axis=0, keepdims=True)


def embed(embeds, basis):
    rows = embeds.shape[0]
    rank = basis.shape[1]
    vmem = pl.BlockSpec(memory_space=pltpu.VMEM)
    return pl.pallas_call(
        embed_kernel,
        in_specs=[vmem] * 2,
        out_specs=[vmem] * 2,
        out_shape=[
            jax.ShapeDtypeStruct((rank, rows), F32),
            jax.ShapeDtypeStruct((1, rows), F32),
        ],
        compiler_params=pltpu.CompilerParams(vmem_limit_bytes=16 * 1024 * 1024),
        name="embed",
    )(embeds, basis)


def join_kernel(part, crossed, out):
    out[0] = part[...]
    out[1] = crossed[...]


def join(part, crossed):
    return pl.pallas_call(
        join_kernel,
        out_shape=jax.ShapeDtypeStruct((2,) + part.shape, part.dtype),
        compiler_params=pltpu.CompilerParams(vmem_limit_bytes=4 * 1024 * 1024),
        name="join",
    )(part, crossed)


def chain_kernel(
    every, norm, emb_basis, cotangent, emb, basis, gain,
    coefs_hbm, kept, sent,
    turned, links, behind, c_kept, g_kept, p_kept, a_kept, pre_kept, slope_kept, coefs, coefs_sem,
):
    count = 2 * every.shape[0]
    width = emb.shape[1]
    inner = 64
    half = lax.axis_index("z_hi")
    core = lax.axis_index("core")
    me = 2 * lax.axis_index("y") + half
    sides = (half, 1 - half)

    def down_of(s):
        return every[s // 2, 0, sides[s % 2], :, :256]

    def up_of(s):
        return every[s // 2, 1, sides[s % 2], :, :256]

    for s in range(count):
        turned[s, 0] = down_of(s).T
        turned[s, 1] = up_of(s).T
    for s in range(1, count):
        links[s, 0] = dot(down_of(s), up_of(s - 1), NT).astype(BF16)
        links[s, 1] = dot(up_of(s - 1), down_of(s), NT).astype(BF16)

    eu = emb_basis[...]
    sq = norm[...]
    c = jnp.zeros(eu.shape, BF16)
    c_kept[0] = c
    invs = []
    base = None
    act = None
    for s in range(count):
        cf = c.astype(F32)
        pre = every[s // 2, core, sides[s % 2], :, 256:].astype(F32)
        total = sq
        if s:
            pre = pre + dot(links[s, 0], act)
            if base is not None:
                pre = pre + base
            hid = eu + cf
            total = total + jnp.sum(cf * (eu + hid), axis=0, keepdims=True)
            behind[s] = dot(up_of(s - 1), hid.astype(BF16))
            if s + 1 < count:
                base = dot(down_of(s + 1), c)
        inv = lax.rsqrt(jnp.maximum(total, 0.0) * (1.0 / width) + EPS)
        invs.append(inv)
        pre = pre * inv
        sig = 1.0 / (1.0 + jnp.exp(-pre))
        act = (pre * sig).astype(BF16)
        pre_kept[s] = pre
        slope_kept[s] = sig * (1.0 + pre * (1.0 - sig))
        a_kept[s] = act
        c = (cf + dot(turned[s, 1], act)).astype(BF16)
        c_kept[s + 1] = c
    coefs[...] = c_kept[me + 1].T
    coefs_copy = pltpu.make_async_copy(coefs, coefs_hbm, coefs_sem)
    coefs_copy.start()

    g = cotangent[...].T
    grad_act = dot(up_of(count - 1), g)
    for s in reversed(range(count)):
        g_kept[s] = g
        inv = invs[s]
        gp = (grad_act * slope_kept[s]).astype(BF16)
        gpf = gp.astype(F32)
        p_kept[s] = (gpf * inv).astype(BF16)
        if s:
            base = dot(up_of(s - 1), g)
            pull = inv * inv * (jnp.sum(gpf * pre_kept[s], axis=0, keepdims=True) * (1.0 / width))
            grad_act = base + inv * dot(links[s, 1], gp) - pull * behind[s]
            hid = eu + c_kept[s].astype(F32)
            g = (g.astype(F32) + inv * dot(turned[s, 0], gp) - pull * hid).astype(BF16)

    p_t = p_kept[me]
    cp = dot(p_t, c_kept[me], NT).astype(BF16)
    s2 = dot(a_kept[me], g_kept[me], NT)
    kept[8] = s2
    sent[8] = s2.astype(BF16)
    low = lax.broadcasted_iota(jnp.int32, (inner, 128), 1) < 64
    first_core = core == 0
    for j in range(8):
        spans = [slice(far * 1024 + j * 128, far * 1024 + j * 128 + 128) for far in range(4)]
        tiles = jnp.concatenate([emb[:, at] for at in spans], axis=1)
        rows = jnp.concatenate([basis[at, :] for at in spans], axis=0)
        scale = jnp.concatenate([gain[:, at] for at in spans], axis=1)
        grad = (dot(p_t, tiles) + dot(cp, rows, NT)) * scale
        for q in range(2):
            one = grad[:, 256 * q : 256 * q + 128]
            two = grad[:, 256 * q + 128 : 256 * q + 256]
            lanes = slice(q * 128, q * 128 + 128)
            zero = jnp.where(low, one, pltpu.roll(two, 64, 1))
            other_half = jnp.where(low, pltpu.roll(one, 64, 1), two)
            kept[j, :, lanes] = jnp.where(first_core, zero, other_half)
            sent[j, :, lanes] = jnp.where(first_core, other_half, zero).astype(BF16)
    coefs_copy.wait()


def chain(every, norm, emb_basis, cotangent, embeds, basis, gain):
    count = 2 * every.shape[0]
    rows, rank = cotangent.shape
    inner = 64
    hbm = pl.BlockSpec(memory_space=pltpu.HBM)
    vmem = pl.BlockSpec(memory_space=pltpu.VMEM)
    return pl.pallas_call(
        chain_kernel,
        in_specs=[vmem] * 7,
        out_specs=[hbm, vmem, vmem],
        out_shape=[
            pltpu.HBM((rows, rank), BF16),
            jax.ShapeDtypeStruct((9, inner, 256), F32),
            jax.ShapeDtypeStruct((9, inner, 256), BF16),
        ],
        scratch_shapes=[
            pltpu.VMEM((count, 2, rank, inner), BF16),
            pltpu.VMEM((count, 2, inner, inner), BF16),
            pltpu.VMEM((count, inner, rows), F32),
            pltpu.VMEM((count + 1, rank, rows), BF16),
            pltpu.VMEM((count, rank, rows), BF16),
            pltpu.VMEM((count, inner, rows), BF16),
            pltpu.VMEM((count, inner, rows), BF16),
            pltpu.VMEM((count, inner, rows), F32),
            pltpu.VMEM((count, inner, rows), F32),
            pltpu.VMEM((rows, rank), BF16),
            pltpu.SemaphoreType.DMA,
        ],
        compiler_params=pltpu.CompilerParams(vmem_limit_bytes=32 * 1024 * 1024),
        name="chain",
    )(every, norm, emb_basis, cotangent, embeds, basis, gain)


def merge_kernel(kept, got, out):
    weights = (kept[8] + got[8].astype(F32)).astype(BF16)
    for j in range(8):
        out[j, :, :256] = (kept[j] + got[j].astype(F32)).astype(BF16)
        out[j, :, 256:] = weights


def merge(kept, got):
    return pl.pallas_call(
        merge_kernel,
        out_shape=jax.ShapeDtypeStruct((8, 64, 512), BF16),
        compiler_params=pltpu.CompilerParams(vmem_limit_bytes=8 * 1024 * 1024),
        name="merge",
    )(kept, got)


def middle_kernel(got, basis, out):
    total = got[0].astype(F32)
    for j in range(1, got.shape[0]):
        total = total + got[j].astype(F32)
    lane = 4 * lax.axis_index("z_near") + lax.axis_index("x")
    rows = basis[:, lane, lax.axis_index("core")].reshape(256, 256)
    w2 = dot(total[:, 256:].astype(BF16), rows, NT)
    both = jnp.concatenate([total[:, :256], w2], axis=0)
    out[...] = both.T.astype(BF16).reshape(out.shape)


def middle(got, basis):
    return pl.pallas_call(
        middle_kernel,
        in_specs=[pl.BlockSpec(memory_space=pltpu.VMEM)] * 2,
        out_specs=pl.BlockSpec(memory_space=pltpu.VMEM),
        out_shape=jax.ShapeDtypeStruct((4, 64, 128), BF16),
        compiler_params=pltpu.CompilerParams(vmem_limit_bytes=16 * 1024 * 1024),
        name="middle",
    )(got, basis.reshape(4, 8, 2, 64, 256))


def final_kernel(got, out):
    total = got[0].astype(F32)
    for j in range(1, got.shape[0]):
        total = total + got[j].astype(F32)
    out[...] = total


def final(got):
    return pl.pallas_call(
        final_kernel,
        out_shape=jax.ShapeDtypeStruct(got.shape[1:], F32),
        compiler_params=pltpu.CompilerParams(vmem_limit_bytes=4 * 1024 * 1024),
        name="final",
    )(got)


def local(embeds, shared_basis, down_proj, up_proj, norm_gain, coef_grad):
    part = project(embeds, shared_basis, down_proj[0].T, up_proj[0].T, norm_gain)
    crossed = lax.ppermute(part, "z_hi", [(0, 1), (1, 0)])
    emb_basis, norm = embed(embeds, shared_basis)
    every = lax.all_gather(join(part, crossed), ("y", "core"), tiled=False)
    every = every.reshape((4, 2, 2) + part.shape)
    coefs, kept, sent = chain(every, norm, emb_basis, coef_grad, embeds, shared_basis, norm_gain)
    got = lax.ppermute(sent, "core", [(0, 1), (1, 0)])
    got = lax.all_to_all(merge(kept, got), ("z_near", "x"), 0, 0, tiled=True)
    got = lax.all_to_all(middle(got, shared_basis), "z_far", 0, 0, tiled=True)
    return coefs[None], final(got)[None]


def solution(mesh):
    fine = Mesh(mesh.devices.reshape(SIZES), AXES)
    placed = (
        P(REPLICA, None),
        P(),
        P(SECTION, None, None),
        P(SECTION, None, None),
        P(SECTION, None),
        P(REPLICA, None),
    )
    return jax.shard_map(
        local,
        mesh=fine,
        in_specs=placed,
        out_specs=(P(SECTION, REPLICA, None), P(SECTION, REPLICA, None)),
        check_vma=False,
    )
```

```python
import functools

import jax
import jax.numpy as jnp
from jax import lax
from jax.experimental import pallas as pl
from jax.experimental.pallas import tpu as pltpu
from jax.sharding import Mesh, PartitionSpec as P

F32 = jnp.float32
BF16 = jnp.bfloat16
EPS = 1e-05
SECTION = ("y", "z_hi")
REPLICA = ("z_far", "z_near", "x", "core")
AXES = SECTION + REPLICA
SIZES = (4, 2, 4, 2, 4, 2)

NN = (((1,), (0,)), ((), ()))
NT = (((1,), (1,)), ((), ()))
TN = (((0,), (0,)), ((), ()))


def dot(a, b, dims=NN):
    return lax.dot_general(a, b, dims, preferred_element_type=F32)


def project_kernel(
    chunk, emb_hbm, basis_hbm, down_hbm, up_hbm, gain_hbm,
    part, emb, basis, down, up, gain, sems,
):
    rows, width = emb.shape
    inner = down.shape[0]
    steps = width // chunk
    gain_copy = pltpu.make_async_copy(gain_hbm, gain, sems.at[4, 0])
    gain_copy.start()
    copies = []
    for i in range(steps):
        at = slice(i * chunk, (i + 1) * chunk)
        group = [
            pltpu.make_async_copy(down_hbm.at[:, at], down.at[:, at], sems.at[0, i]),
            pltpu.make_async_copy(up_hbm.at[:, at], up.at[:, at], sems.at[1, i]),
            pltpu.make_async_copy(emb_hbm.at[:, at], emb.at[:, at], sems.at[2, i]),
            pltpu.make_async_copy(basis_hbm.at[at, :], basis.at[at, :], sems.at[3, i]),
        ]
        for copy in group:
            copy.start()
        copies.append(group)
    gain_copy.wait()
    acc = jnp.zeros((2 * inner, basis.shape[1]), F32)
    pre = jnp.zeros((inner, rows), F32)
    for i in range(steps):
        at = slice(i * chunk, (i + 1) * chunk)
        for copy in copies[i]:
            copy.wait()
        scaled = (down[:, at].astype(F32) * gain[:, at]).astype(BF16)
        acc = acc + dot(jnp.concatenate([scaled, up[:, at]], axis=0), basis[at, :])
        pre = pre + dot(scaled, emb[:, at], NT)
    first = lax.axis_index("core") == 0
    part[:, :256] = jnp.where(first, acc[:inner], acc[inner:]).astype(BF16)
    part[:, 256:] = pre.astype(BF16)


def project(embeds, basis, down_t, up_t, gain):
    rows, width = embeds.shape
    rank = basis.shape[1]
    inner = down_t.shape[0]
    chunk = 1024
    args = [pltpu.with_memory_space_constraint(a, pltpu.HBM) for a in (embeds, basis, down_t, up_t, gain)]
    return pl.pallas_call(
        functools.partial(project_kernel, chunk),
        in_specs=[pl.BlockSpec(memory_space=pltpu.HBM)] * 5,
        out_specs=pl.BlockSpec(memory_space=pltpu.VMEM),
        out_shape=jax.ShapeDtypeStruct((inner, rank + rows), BF16),
        scratch_shapes=[
            pltpu.VMEM((rows, width), BF16),
            pltpu.VMEM((width, rank), BF16),
            pltpu.VMEM((inner, width), BF16),
            pltpu.VMEM((inner, width), BF16),
            pltpu.VMEM((1, width), F32),
            pltpu.SemaphoreType.DMA((5, width // chunk)),
        ],
        compiler_params=pltpu.CompilerParams(vmem_limit_bytes=24 * 1024 * 1024),
        name="project",
    )(*args)


def embed_kernel(emb, basis, gain, cotangent, after, emb_basis, norm, mine, gain_mine, share_wide, share):
    del after
    rows, width = emb.shape
    chunk = 1024
    acc = jnp.zeros((rows, basis.shape[1]), F32)
    square = jnp.zeros((rows, 128), F32)
    for at in range(0, width, chunk):
        e = emb[:, at : at + chunk]
        acc = acc + dot(e, basis[at : at + chunk, :])
        ef = e.astype(F32)
        sq = ef * ef
        for k in range(0, chunk, 128):
            square = square + sq[:, k : k + 128]
    emb_basis[...] = acc.T
    norm[...] = jnp.sum(square.T, axis=0, keepdims=True)
    high = acc.astype(BF16)
    share[:, 512:768] = high
    share[:, 768:1024] = (acc - high.astype(F32)).astype(BF16)
    share[:, 1024:1280] = cotangent[...]
    total = jnp.broadcast_to(jnp.sum(square, axis=1, keepdims=True), (rows, 128))
    first = total.astype(BF16).astype(F32)
    second = (total - first).astype(BF16).astype(F32)
    lane = lax.broadcasted_iota(jnp.int32, (rows, 128), 1)
    parts = jnp.where(lane == 0, first, jnp.where(lane == 1, second, total - first - second))
    share[:, 1280:1408] = parts.astype(BF16)
    even = lax.axis_index("core") == 0
    for j in range(8):
        for q in range(2):
            one = slice(2048 * q + j * 128, 2048 * q + j * 128 + 128)
            two = slice(2048 * q + 1024 + j * 128, 2048 * q + 1024 + j * 128 + 128)
            lanes = slice(j * 256 + q * 128, j * 256 + q * 128 + 128)
            for source, target, rest in ((emb, mine, share), (gain, gain_mine, None)):
                left = source[:, one].astype(F32)
                right = source[:, two].astype(F32)
                low = lax.broadcasted_iota(jnp.int32, left.shape, 1) < 64
                zero = jnp.where(low, left, pltpu.roll(right, 64, 1))
                other = jnp.where(low, pltpu.roll(left, 64, 1), right)
                target[:, lanes] = jnp.where(even, zero, other).astype(target.dtype)
                if rest is not None and j < 6:
                    share_wide[:, lanes] = jnp.where(even, other, zero).astype(rest.dtype)
                elif rest is not None:
                    rest[:, lanes.start - 1536 : lanes.stop - 1536] = jnp.where(even, other, zero).astype(rest.dtype)


def embed(embeds, basis, gain, cotangent, after):
    rows, width = embeds.shape
    rank = basis.shape[1]
    vmem = pl.BlockSpec(memory_space=pltpu.VMEM)
    return pl.pallas_call(
        embed_kernel,
        in_specs=[vmem] * 4 + [pl.BlockSpec(memory_space=pl.ANY)],
        out_specs=[vmem] * 6,
        out_shape=[
            jax.ShapeDtypeStruct((rank, rows), F32),
            jax.ShapeDtypeStruct((1, rows), F32),
            jax.ShapeDtypeStruct((rows, width // 2), BF16),
            jax.ShapeDtypeStruct((1, width // 2), F32),
            jax.ShapeDtypeStruct((rows, 1536), BF16),
            jax.ShapeDtypeStruct((rows, width // 2 - 1536 + 3 * rank + 128), BF16),
        ],
        compiler_params=pltpu.CompilerParams(vmem_limit_bytes=16 * 1024 * 1024),
        name="embed",
    )(embeds, basis, gain, cotangent, after)


def join_kernel(part, crossed, out):
    out[0] = part[...]
    out[1] = crossed[...]


def join(part, crossed):
    return pl.pallas_call(
        join_kernel,
        out_shape=jax.ShapeDtypeStruct((2,) + part.shape, part.dtype),
        compiler_params=pltpu.CompilerParams(vmem_limit_bytes=4 * 1024 * 1024),
        name="join",
    )(part, crossed)


def chain_kernel(
    every, norm, emb_basis, cotangent, mine, basis, gain, share_wide, share,
    coefs_hbm, slots,
    turned, links, behind, c_kept, g_kept, p_kept, a_kept, pre_kept, slope_kept, coefs, coefs_sem,
):
    count = 2 * every.shape[0]
    rows, width = mine.shape[0], 2 * mine.shape[1]
    inner = 64
    half = lax.axis_index("z_hi")
    core = lax.axis_index("core")
    me = 2 * lax.axis_index("y") + half
    sides = (half, 1 - half)

    def down_of(s):
        return every[s // 2, 0, sides[s % 2], :, :256]

    def up_of(s):
        return every[s // 2, 1, sides[s % 2], :, :256]

    for s in range(count):
        turned[s, 0] = down_of(s).T
        turned[s, 1] = up_of(s).T
    for s in range(1, count):
        links[s, 0] = dot(down_of(s), up_of(s - 1), NT).astype(BF16)
        links[s, 1] = dot(up_of(s - 1), down_of(s), NT).astype(BF16)

    theirs = (share[:, 512:768].astype(F32) + share[:, 768:1024].astype(F32)).T
    parts = share[:, 1280:1408].astype(F32).T
    eu = jnp.concatenate([emb_basis[...], theirs], axis=1)
    sq = jnp.concatenate([norm[...], parts[0:1] + parts[1:2] + parts[2:3]], axis=1)
    c = jnp.zeros(eu.shape, BF16)
    c_kept[0] = c
    invs = []
    base = None
    act = None
    for s in range(count):
        cf = c.astype(F32)
        pre = jnp.concatenate(
            [every[s // 2, k, sides[s % 2], :, 256:].astype(F32) for k in (core, 1 - core)], axis=1
        )
        total = sq
        if s:
            pre = pre + dot(links[s, 0], act)
            if base is not None:
                pre = pre + base
            hid = eu + cf
            total = total + jnp.sum(cf * (eu + hid), axis=0, keepdims=True)
            behind[s] = dot(up_of(s - 1), hid.astype(BF16))
            if s + 1 < count:
                base = dot(down_of(s + 1), c)
        inv = lax.rsqrt(jnp.maximum(total, 0.0) * (1.0 / width) + EPS)
        invs.append(inv)
        pre = pre * inv
        sig = 1.0 / (1.0 + jnp.exp(-pre))
        act = (pre * sig).astype(BF16)
        pre_kept[s] = pre
        slope_kept[s] = sig * (1.0 + pre * (1.0 - sig))
        a_kept[s] = act
        c = (cf + dot(turned[s, 1], act)).astype(BF16)
        c_kept[s + 1] = c
    coefs[...] = c_kept[me + 1, :, :rows].T
    coefs_copy = pltpu.make_async_copy(coefs, coefs_hbm, coefs_sem)
    coefs_copy.start()

    g = jnp.concatenate([cotangent[...].T, share[:, 1024:1280].T], axis=1)
    grad_act = dot(up_of(count - 1), g)
    for s in reversed(range(count)):
        g_kept[s] = g
        inv = invs[s]
        gp = (grad_act * slope_kept[s]).astype(BF16)
        gpf = gp.astype(F32)
        p_kept[s] = (gpf * inv).astype(BF16)
        if s:
            base = dot(up_of(s - 1), g)
            pull = inv * inv * (jnp.sum(gpf * pre_kept[s], axis=0, keepdims=True) * (1.0 / width))
            grad_act = base + inv * dot(links[s, 1], gp) - pull * behind[s]
            hid = eu + c_kept[s].astype(F32)
            g = (g.astype(F32) + inv * dot(turned[s, 0], gp) - pull * hid).astype(BF16)

    p_t = p_kept[me]
    cp = dot(p_t, c_kept[me], NT).astype(BF16)
    s2 = dot(a_kept[me], g_kept[me], NT).astype(BF16)
    for j in range(8):
        lanes = slice(j * 256, j * 256 + 256)
        rest = share_wide[:, lanes] if j < 6 else share[:, j * 256 - 1536 : j * 256 - 1280]
        tokens = jnp.concatenate([mine[:, lanes], rest], axis=0)
        spans = jnp.concatenate([basis[far, j, core] for far in range(4)], axis=0)
        slots[j, :, :256] = ((dot(p_t, tokens) + dot(cp, spans, NT)) * gain[:, lanes]).astype(BF16)
        slots[j, :, 256:] = s2
    coefs_copy.wait()


def chain(every, norm, emb_basis, cotangent, mine, basis, gain, share_wide, share):
    count = 2 * every.shape[0]
    rows, rank = cotangent.shape
    tokens = 2 * rows
    inner = 64
    hbm = pl.BlockSpec(memory_space=pltpu.HBM)
    vmem = pl.BlockSpec(memory_space=pltpu.VMEM)
    return pl.pallas_call(
        chain_kernel,
        in_specs=[vmem] * 9,
        out_specs=[hbm, vmem],
        out_shape=[
            pltpu.HBM((rows, rank), BF16),
            jax.ShapeDtypeStruct((8, inner, 2 * rank), BF16),
        ],
        scratch_shapes=[
            pltpu.VMEM((count, 2, rank, inner), BF16),
            pltpu.VMEM((count, 2, inner, inner), BF16),
            pltpu.VMEM((count, inner, tokens), F32),
            pltpu.VMEM((count + 1, rank, tokens), BF16),
            pltpu.VMEM((count, rank, tokens), BF16),
            pltpu.VMEM((count, inner, tokens), BF16),
            pltpu.VMEM((count, inner, tokens), BF16),
            pltpu.VMEM((count, inner, tokens), F32),
            pltpu.VMEM((count, inner, tokens), F32),
            pltpu.VMEM((rows, rank), BF16),
            pltpu.SemaphoreType.DMA,
        ],
        compiler_params=pltpu.CompilerParams(vmem_limit_bytes=32 * 1024 * 1024),
        name="chain",
    )(every, norm, emb_basis, cotangent, mine, basis.reshape(4, 8, 2, 64, 256), gain, share_wide, share)


def middle_kernel(got, basis, out):
    total = got[0].astype(F32)
    for j in range(1, got.shape[0]):
        total = total + got[j].astype(F32)
    lane = 4 * lax.axis_index("z_near") + lax.axis_index("x")
    rows = basis[:, lane, lax.axis_index("core")].reshape(256, 256)
    w2 = dot(total[:, 256:].astype(BF16), rows, NT)
    both = jnp.concatenate([total[:, :256], w2], axis=0)
    out[...] = both.T.astype(BF16).reshape(out.shape)


def middle(got, basis):
    return pl.pallas_call(
        middle_kernel,
        in_specs=[pl.BlockSpec(memory_space=pltpu.VMEM)] * 2,
        out_specs=pl.BlockSpec(memory_space=pltpu.VMEM),
        out_shape=jax.ShapeDtypeStruct((4, 64, 128), BF16),
        compiler_params=pltpu.CompilerParams(vmem_limit_bytes=16 * 1024 * 1024),
        name="middle",
    )(got, basis.reshape(4, 8, 2, 64, 256))


def final_kernel(got, out):
    total = got[0].astype(F32)
    for j in range(1, got.shape[0]):
        total = total + got[j].astype(F32)
    out[...] = total


def final(got):
    return pl.pallas_call(
        final_kernel,
        out_shape=jax.ShapeDtypeStruct(got.shape[1:], F32),
        compiler_params=pltpu.CompilerParams(vmem_limit_bytes=4 * 1024 * 1024),
        name="final",
    )(got)


def local(embeds, shared_basis, down_proj, up_proj, norm_gain, coef_grad):
    part = project(embeds, shared_basis, down_proj[0].T, up_proj[0].T, norm_gain)
    crossed = lax.ppermute(part, "z_hi", [(0, 1), (1, 0)])
    emb_basis, norm, mine, gain, share_wide, share = embed(embeds, shared_basis, norm_gain, coef_grad, part)
    share_wide = lax.ppermute(share_wide, "core", [(0, 1), (1, 0)])
    share = lax.ppermute(share, "core", [(0, 1), (1, 0)])
    every = lax.all_gather(join(part, crossed), ("y", "core"), tiled=False)
    every = every.reshape((4, 2, 2) + part.shape)
    coefs, slots = chain(every, norm, emb_basis, coef_grad, mine, shared_basis, gain, share_wide, share)
    got = lax.all_to_all(slots, ("z_near", "x"), 0, 0, tiled=True)
    got = lax.all_to_all(middle(got, shared_basis), "z_far", 0, 0, tiled=True)
    return coefs[None], final(got)[None]


def solution(mesh):
    fine = Mesh(mesh.devices.reshape(SIZES), AXES)
    placed = (
        P(REPLICA, None),
        P(),
        P(SECTION, None, None),
        P(SECTION, None, None),
        P(SECTION, None),
        P(REPLICA, None),
    )
    return jax.shard_map(
        local,
        mesh=fine,
        in_specs=placed,
        out_specs=(P(SECTION, REPLICA, None), P(SECTION, REPLICA, None)),
        check_vma=False,
    )
```

```python
import functools

import jax
import jax.numpy as jnp
from jax import lax
from jax.experimental import pallas as pl
from jax.experimental.pallas import tpu as pltpu
from jax.sharding import Mesh, PartitionSpec as P

F32 = jnp.float32
BF16 = jnp.bfloat16
EPS = 1e-05
SECTION = ("y", "z_hi")
REPLICA = ("z_far", "z_near", "x", "core")
AXES = SECTION + REPLICA
SIZES = (4, 2, 4, 2, 4, 2)

NN = (((1,), (0,)), ((), ()))
NT = (((1,), (1,)), ((), ()))
TN = (((0,), (0,)), ((), ()))


def dot(a, b, dims=NN):
    return lax.dot_general(a, b, dims, preferred_element_type=F32)


def project_kernel(
    sizes, emb_hbm, basis_hbm, down_hbm, up_hbm, gain_hbm,
    part, emb, basis, down, up, gain, sems,
):
    rows, width = emb.shape
    inner = down.shape[0]
    half = pl.ds(pl.multiple_of(lax.axis_index("core") * 128, 128), 128)
    gain_copy = pltpu.make_async_copy(gain_hbm, gain, sems.at[4, 0])
    gain_copy.start()
    spans, copies = [], []
    begin = 0
    for i, size in enumerate(sizes):
        at = slice(begin, begin + size)
        begin += size
        group = [
            pltpu.make_async_copy(basis_hbm.at[at, half], basis.at[at, :], sems.at[3, i]),
            pltpu.make_async_copy(emb_hbm.at[:, at], emb.at[:, at], sems.at[2, i]),
            pltpu.make_async_copy(down_hbm.at[:, at], down.at[:, at], sems.at[0, i]),
            pltpu.make_async_copy(up_hbm.at[:, at], up.at[:, at], sems.at[1, i]),
        ]
        for copy in group:
            copy.start()
        spans.append(at)
        copies.append(group)
    gain_copy.wait()
    acc = jnp.zeros((2 * inner, 128), F32)
    pre = jnp.zeros((inner, rows), F32)
    for at, group in zip(spans, copies):
        for copy in group:
            copy.wait()
        scaled = (down[:, at].astype(F32) * gain[:, at]).astype(BF16)
        acc = acc + dot(jnp.concatenate([scaled, up[:, at]], axis=0), basis[at, :])
        pre = pre + dot(scaled, emb[:, at], NT)
    part[:, :128] = acc[:inner].astype(BF16)
    part[:, 128:256] = acc[inner:].astype(BF16)
    part[:, 256:] = pre.astype(BF16)


def project(embeds, basis, down_t, up_t, gain):
    rows, width = embeds.shape
    rank = basis.shape[1]
    inner = down_t.shape[0]
    sizes = (1024,) * 4
    args = [pltpu.with_memory_space_constraint(a, pltpu.HBM) for a in (embeds, basis, down_t, up_t, gain)]
    return pl.pallas_call(
        functools.partial(project_kernel, sizes),
        in_specs=[pl.BlockSpec(memory_space=pltpu.HBM)] * 5,
        out_specs=pl.BlockSpec(memory_space=pltpu.VMEM),
        out_shape=jax.ShapeDtypeStruct((inner, rank + rows), BF16),
        scratch_shapes=[
            pltpu.VMEM((rows, width), BF16),
            pltpu.VMEM((width, 128), BF16),
            pltpu.VMEM((inner, width), BF16),
            pltpu.VMEM((inner, width), BF16),
            pltpu.VMEM((1, width), F32),
            pltpu.SemaphoreType.DMA((5, len(sizes))),
        ],
        compiler_params=pltpu.CompilerParams(vmem_limit_bytes=24 * 1024 * 1024),
        name="project",
    )(*args)


def embed_kernel(emb, basis, gain, cotangent, after, emb_basis, norm, mine, gain_mine, share_wide, share):
    del after
    rows, width = emb.shape
    chunk = 1024
    acc = jnp.zeros((rows, basis.shape[1]), F32)
    square = jnp.zeros((rows, 128), F32)
    for at in range(0, width, chunk):
        e = emb[:, at : at + chunk]
        acc = acc + dot(e, basis[at : at + chunk, :])
        ef = e.astype(F32)
        sq = ef * ef
        for k in range(0, chunk, 128):
            square = square + sq[:, k : k + 128]
    emb_basis[...] = acc.T
    norm[...] = jnp.sum(square.T, axis=0, keepdims=True)
    high = acc.astype(BF16)
    share[:, 512:768] = high
    share[:, 768:1024] = (acc - high.astype(F32)).astype(BF16)
    share[:, 1024:1280] = cotangent[...]
    total = jnp.broadcast_to(jnp.sum(square, axis=1, keepdims=True), (rows, 128))
    first = total.astype(BF16).astype(F32)
    second = (total - first).astype(BF16).astype(F32)
    lane = lax.broadcasted_iota(jnp.int32, (rows, 128), 1)
    parts = jnp.where(lane == 0, first, jnp.where(lane == 1, second, total - first - second))
    share[:, 1280:1408] = parts.astype(BF16)
    even = lax.axis_index("core") == 0
    for j in range(8):
        for q in range(2):
            one = slice(2048 * q + j * 128, 2048 * q + j * 128 + 128)
            two = slice(2048 * q + 1024 + j * 128, 2048 * q + 1024 + j * 128 + 128)
            lanes = slice(j * 256 + q * 128, j * 256 + q * 128 + 128)
            for source, target, rest in ((emb, mine, share), (gain, gain_mine, None)):
                left = source[:, one].astype(F32)
                right = source[:, two].astype(F32)
                low = lax.broadcasted_iota(jnp.int32, left.shape, 1) < 64
                zero = jnp.where(low, left, pltpu.roll(right, 64, 1))
                other = jnp.where(low, pltpu.roll(left, 64, 1), right)
                target[:, lanes] = jnp.where(even, zero, other).astype(target.dtype)
                if rest is not None and j < 6:
                    share_wide[:, lanes] = jnp.where(even, other, zero).astype(rest.dtype)
                elif rest is not None:
                    rest[:, lanes.start - 1536 : lanes.stop - 1536] = jnp.where(even, other, zero).astype(rest.dtype)


def embed(embeds, basis, gain, cotangent, after):
    rows, width = embeds.shape
    rank = basis.shape[1]
    vmem = pl.BlockSpec(memory_space=pltpu.VMEM)
    return pl.pallas_call(
        embed_kernel,
        in_specs=[vmem] * 4 + [pl.BlockSpec(memory_space=pl.ANY)],
        out_specs=[vmem] * 6,
        out_shape=[
            jax.ShapeDtypeStruct((rank, rows), F32),
            jax.ShapeDtypeStruct((1, rows), F32),
            jax.ShapeDtypeStruct((rows, width // 2), BF16),
            jax.ShapeDtypeStruct((1, width // 2), F32),
            jax.ShapeDtypeStruct((rows, 1536), BF16),
            jax.ShapeDtypeStruct((rows, width // 2 - 1536 + 3 * rank + 128), BF16),
        ],
        compiler_params=pltpu.CompilerParams(vmem_limit_bytes=16 * 1024 * 1024),
        name="embed",
    )(embeds, basis, gain, cotangent, after)


def join_kernel(part, crossed, out):
    out[0] = part[...]
    out[1] = crossed[...]


def join(part, crossed):
    return pl.pallas_call(
        join_kernel,
        out_shape=jax.ShapeDtypeStruct((2,) + part.shape, part.dtype),
        compiler_params=pltpu.CompilerParams(vmem_limit_bytes=4 * 1024 * 1024),
        name="join",
    )(part, crossed)


def chain_kernel(
    every, norm, emb_basis, cotangent, mine, basis, gain, share_wide, share,
    coefs_hbm, slots,
    turned, links, behind, c_kept, g_kept, p_kept, a_kept, pre_kept, slope_kept, coefs, coefs_sem,
):
    count = 2 * every.shape[0]
    rows, width = mine.shape[0], 2 * mine.shape[1]
    inner = 64
    half = lax.axis_index("z_hi")
    core = lax.axis_index("core")
    me = 2 * lax.axis_index("y") + half
    sides = (half, 1 - half)

    def down_of(s):
        return jnp.concatenate([every[s // 2, k, sides[s % 2], :, :128] for k in range(2)], axis=1)

    def up_of(s):
        return jnp.concatenate([every[s // 2, k, sides[s % 2], :, 128:256] for k in range(2)], axis=1)

    for s in range(count):
        turned[s, 0] = down_of(s).T
        turned[s, 1] = up_of(s).T
    for s in range(1, count):
        links[s, 0] = dot(down_of(s), up_of(s - 1), NT).astype(BF16)
        links[s, 1] = dot(up_of(s - 1), down_of(s), NT).astype(BF16)

    theirs = (share[:, 512:768].astype(F32) + share[:, 768:1024].astype(F32)).T
    parts = share[:, 1280:1408].astype(F32).T
    eu = jnp.concatenate([emb_basis[...], theirs], axis=1)
    sq = jnp.concatenate([norm[...], parts[0:1] + parts[1:2] + parts[2:3]], axis=1)
    c = jnp.zeros(eu.shape, BF16)
    c_kept[0] = c
    invs = []
    base = None
    act = None
    for s in range(count):
        cf = c.astype(F32)
        pre = jnp.concatenate(
            [every[s // 2, k, sides[s % 2], :, 256:].astype(F32) for k in (core, 1 - core)], axis=1
        )
        total = sq
        if s:
            pre = pre + dot(links[s, 0], act)
            if base is not None:
                pre = pre + base
            hid = eu + cf
            total = total + jnp.sum(cf * (eu + hid), axis=0, keepdims=True)
            behind[s] = dot(up_of(s - 1), hid.astype(BF16))
            if s + 1 < count:
                base = dot(down_of(s + 1), c)
        inv = lax.rsqrt(jnp.maximum(total, 0.0) * (1.0 / width) + EPS)
        invs.append(inv)
        pre = pre * inv
        sig = 1.0 / (1.0 + jnp.exp(-pre))
        act = (pre * sig).astype(BF16)
        pre_kept[s] = pre
        slope_kept[s] = sig * (1.0 + pre * (1.0 - sig))
        a_kept[s] = act
        c = (cf + dot(turned[s, 1], act)).astype(BF16)
        c_kept[s + 1] = c
    coefs[...] = c_kept[me + 1, :, :rows].T
    coefs_copy = pltpu.make_async_copy(coefs, coefs_hbm, coefs_sem)
    coefs_copy.start()

    g = jnp.concatenate([cotangent[...].T, share[:, 1024:1280].T], axis=1)
    grad_act = dot(up_of(count - 1), g)
    for s in reversed(range(count)):
        g_kept[s] = g
        inv = invs[s]
        gp = (grad_act * slope_kept[s]).astype(BF16)
        gpf = gp.astype(F32)
        p_kept[s] = (gpf * inv).astype(BF16)
        if s:
            base = dot(up_of(s - 1), g)
            pull = inv * inv * (jnp.sum(gpf * pre_kept[s], axis=0, keepdims=True) * (1.0 / width))
            grad_act = base + inv * dot(links[s, 1], gp) - pull * behind[s]
            hid = eu + c_kept[s].astype(F32)
            g = (g.astype(F32) + inv * dot(turned[s, 0], gp) - pull * hid).astype(BF16)

    p_t = p_kept[me]
    cp = dot(p_t, c_kept[me], NT).astype(BF16)
    s2 = dot(a_kept[me], g_kept[me], NT).astype(BF16)
    for j in range(8):
        lanes = slice(j * 256, j * 256 + 256)
        rest = share_wide[:, lanes] if j < 6 else share[:, j * 256 - 1536 : j * 256 - 1280]
        tokens = jnp.concatenate([mine[:, lanes], rest], axis=0)
        spans = jnp.concatenate([basis[far, j, core] for far in range(4)], axis=0)
        slots[j, :, :256] = ((dot(p_t, tokens) + dot(cp, spans, NT)) * gain[:, lanes]).astype(BF16)
        slots[j, :, 256:] = s2
    coefs_copy.wait()


def chain(every, norm, emb_basis, cotangent, mine, basis, gain, share_wide, share):
    count = 2 * every.shape[0]
    rows, rank = cotangent.shape
    tokens = 2 * rows
    inner = 64
    hbm = pl.BlockSpec(memory_space=pltpu.HBM)
    vmem = pl.BlockSpec(memory_space=pltpu.VMEM)
    return pl.pallas_call(
        chain_kernel,
        in_specs=[vmem] * 9,
        out_specs=[hbm, vmem],
        out_shape=[
            pltpu.HBM((rows, rank), BF16),
            jax.ShapeDtypeStruct((8, inner, 2 * rank), BF16),
        ],
        scratch_shapes=[
            pltpu.VMEM((count, 2, rank, inner), BF16),
            pltpu.VMEM((count, 2, inner, inner), BF16),
            pltpu.VMEM((count, inner, tokens), F32),
            pltpu.VMEM((count + 1, rank, tokens), BF16),
            pltpu.VMEM((count, rank, tokens), BF16),
            pltpu.VMEM((count, inner, tokens), BF16),
            pltpu.VMEM((count, inner, tokens), BF16),
            pltpu.VMEM((count, inner, tokens), F32),
            pltpu.VMEM((count, inner, tokens), F32),
            pltpu.VMEM((rows, rank), BF16),
            pltpu.SemaphoreType.DMA,
        ],
        compiler_params=pltpu.CompilerParams(vmem_limit_bytes=32 * 1024 * 1024),
        name="chain",
    )(every, norm, emb_basis, cotangent, mine, basis.reshape(4, 8, 2, 64, 256), gain, share_wide, share)


def middle_kernel(got, basis, out):
    total = got[0].astype(F32)
    for j in range(1, got.shape[0]):
        total = total + got[j].astype(F32)
    lane = 4 * lax.axis_index("z_near") + lax.axis_index("x")
    rows = basis[:, lane, lax.axis_index("core")].reshape(256, 256)
    w2 = dot(total[:, 256:].astype(BF16), rows, NT)
    both = jnp.concatenate([total[:, :256], w2], axis=0)
    out[...] = both.T.astype(BF16).reshape(out.shape)


def middle(got, basis):
    return pl.pallas_call(
        middle_kernel,
        in_specs=[pl.BlockSpec(memory_space=pltpu.VMEM)] * 2,
        out_specs=pl.BlockSpec(memory_space=pltpu.VMEM),
        out_shape=jax.ShapeDtypeStruct((4, 64, 128), BF16),
        compiler_params=pltpu.CompilerParams(vmem_limit_bytes=16 * 1024 * 1024),
        name="middle",
    )(got, basis.reshape(4, 8, 2, 64, 256))


def final_kernel(got, out):
    total = got[0].astype(F32)
    for j in range(1, got.shape[0]):
        total = total + got[j].astype(F32)
    out[...] = total


def final(got):
    return pl.pallas_call(
        final_kernel,
        out_shape=jax.ShapeDtypeStruct(got.shape[1:], F32),
        compiler_params=pltpu.CompilerParams(vmem_limit_bytes=4 * 1024 * 1024),
        name="final",
    )(got)


def local(embeds, shared_basis, down_proj, up_proj, norm_gain, coef_grad):
    part = project(embeds, shared_basis, down_proj[0].T, up_proj[0].T, norm_gain)
    crossed = lax.ppermute(part, "z_hi", [(0, 1), (1, 0)])
    emb_basis, norm, mine, gain, share_wide, share = embed(embeds, shared_basis, norm_gain, coef_grad, part)
    share_wide = lax.ppermute(share_wide, "core", [(0, 1), (1, 0)])
    share = lax.ppermute(share, "core", [(0, 1), (1, 0)])
    every = lax.all_gather(join(part, crossed), ("y", "core"), tiled=False)
    every = every.reshape((4, 2, 2) + part.shape)
    coefs, slots = chain(every, norm, emb_basis, coef_grad, mine, shared_basis, gain, share_wide, share)
    got = lax.all_to_all(slots, ("z_near", "x"), 0, 0, tiled=True)
    got = lax.all_to_all(middle(got, shared_basis), "z_far", 0, 0, tiled=True)
    return coefs[None], final(got)[None]


def solution(mesh):
    fine = Mesh(mesh.devices.reshape(SIZES), AXES)
    placed = (
        P(REPLICA, None),
        P(),
        P(SECTION, None, None),
        P(SECTION, None, None),
        P(SECTION, None),
        P(REPLICA, None),
    )
    return jax.shard_map(
        local,
        mesh=fine,
        in_specs=placed,
        out_specs=(P(SECTION, REPLICA, None), P(SECTION, REPLICA, None)),
        check_vma=False,
    )
```

```python
import functools

import jax
import jax.numpy as jnp
from jax import lax
from jax.experimental import pallas as pl
from jax.experimental.pallas import tpu as pltpu
from jax.sharding import Mesh, PartitionSpec as P

F32 = jnp.float32
BF16 = jnp.bfloat16
EPS = 1e-05
SECTION = ("y", "z_hi")
REPLICA = ("z_far", "z_near", "x", "core")
AXES = SECTION + REPLICA
SIZES = (4, 2, 4, 2, 4, 2)

NN = (((1,), (0,)), ((), ()))
NT = (((1,), (1,)), ((), ()))
TN = (((0,), (0,)), ((), ()))


def dot(a, b, dims=NN):
    return lax.dot_general(a, b, dims, preferred_element_type=F32)


def project_kernel(
    sizes, emb_hbm, basis_hbm, down_hbm, up_hbm, gain_hbm,
    part, emb, basis, down, up, gain, sems,
):
    rows, width = emb.shape
    inner = down.shape[0]
    half = pl.ds(pl.multiple_of(lax.axis_index("core") * 128, 128), 128)
    gain_copy = pltpu.make_async_copy(gain_hbm, gain, sems.at[4, 0])
    gain_copy.start()
    spans, copies = [], []
    begin = 0
    for i, size in enumerate(sizes):
        at = slice(begin, begin + size)
        begin += size
        group = [
            pltpu.make_async_copy(basis_hbm.at[at, half], basis.at[at, :], sems.at[3, i]),
            pltpu.make_async_copy(emb_hbm.at[:, at], emb.at[:, at], sems.at[2, i]),
            pltpu.make_async_copy(down_hbm.at[:, at], down.at[:, at], sems.at[0, i]),
            pltpu.make_async_copy(up_hbm.at[:, at], up.at[:, at], sems.at[1, i]),
        ]
        for copy in group:
            copy.start()
        spans.append(at)
        copies.append(group)
    gain_copy.wait()
    acc = jnp.zeros((2 * inner, 128), F32)
    pre = jnp.zeros((inner, rows), F32)
    for at, group in zip(spans, copies):
        for copy in group:
            copy.wait()
        scaled = (down[:, at].astype(F32) * gain[:, at]).astype(BF16)
        acc = acc + dot(jnp.concatenate([scaled, up[:, at]], axis=0), basis[at, :])
        pre = pre + dot(scaled, emb[:, at], NT)
    part[:, :128] = acc[:inner].astype(BF16)
    part[:, 128:256] = acc[inner:].astype(BF16)
    part[:, 256:] = pre.astype(BF16)


def project(embeds, basis, down_t, up_t, gain):
    rows, width = embeds.shape
    rank = basis.shape[1]
    inner = down_t.shape[0]
    sizes = (1024,) * 4
    args = [pltpu.with_memory_space_constraint(a, pltpu.HBM) for a in (embeds, basis, down_t, up_t, gain)]
    return pl.pallas_call(
        functools.partial(project_kernel, sizes),
        in_specs=[pl.BlockSpec(memory_space=pltpu.HBM)] * 5,
        out_specs=pl.BlockSpec(memory_space=pltpu.VMEM),
        out_shape=jax.ShapeDtypeStruct((inner, rank + rows), BF16),
        scratch_shapes=[
            pltpu.VMEM((rows, width), BF16),
            pltpu.VMEM((width, 128), BF16),
            pltpu.VMEM((inner, width), BF16),
            pltpu.VMEM((inner, width), BF16),
            pltpu.VMEM((1, width), F32),
            pltpu.SemaphoreType.DMA((5, len(sizes))),
        ],
        compiler_params=pltpu.CompilerParams(vmem_limit_bytes=24 * 1024 * 1024),
        name="project",
    )(*args)


def embed_kernel(emb, basis, gain, cotangent, after, emb_basis, norm, cot_turned, mine, gain_mine, share_wide, share):
    del after
    rows, width = emb.shape
    chunk = 1024
    acc = jnp.zeros((rows, basis.shape[1]), F32)
    square = jnp.zeros((rows, 128), F32)
    for at in range(0, width, chunk):
        e = emb[:, at : at + chunk]
        acc = acc + dot(e, basis[at : at + chunk, :])
        ef = e.astype(F32)
        sq = ef * ef
        for k in range(0, chunk, 128):
            square = square + sq[:, k : k + 128]
    turned = acc.T
    emb_basis[...] = turned
    high = turned.astype(BF16)
    low_part = (turned - high.astype(F32)).astype(BF16)
    cot = cotangent[...].T
    cot_turned[...] = cot
    for begin, whole in ((512, high), (768, low_part), (1024, cot)):
        share[:, begin : begin + 128] = whole[:rows]
        share[:, begin + 128 : begin + 256] = whole[rows:]
    total = jnp.sum(square.T, axis=0, keepdims=True)
    norm[...] = total
    total = jnp.broadcast_to(total, (rows, 128))
    first = total.astype(BF16).astype(F32)
    second = (total - first).astype(BF16).astype(F32)
    row = lax.broadcasted_iota(jnp.int32, (rows, 128), 0)
    parts = jnp.where(row == 0, first, jnp.where(row == 1, second, total - first - second))
    share[:, 1280:1408] = parts.astype(BF16)
    even = lax.axis_index("core") == 0
    for j in range(8):
        for q in range(2):
            one = slice(2048 * q + j * 128, 2048 * q + j * 128 + 128)
            two = slice(2048 * q + 1024 + j * 128, 2048 * q + 1024 + j * 128 + 128)
            lanes = slice(j * 256 + q * 128, j * 256 + q * 128 + 128)
            for source, target, rest in ((emb, mine, share), (gain, gain_mine, None)):
                left = source[:, one].astype(F32)
                right = source[:, two].astype(F32)
                low = lax.broadcasted_iota(jnp.int32, left.shape, 1) < 64
                zero = jnp.where(low, left, pltpu.roll(right, 64, 1))
                other = jnp.where(low, pltpu.roll(left, 64, 1), right)
                target[:, lanes] = jnp.where(even, zero, other).astype(target.dtype)
                if rest is not None and j < 6:
                    share_wide[:, lanes] = jnp.where(even, other, zero).astype(rest.dtype)
                elif rest is not None:
                    rest[:, lanes.start - 1536 : lanes.stop - 1536] = jnp.where(even, other, zero).astype(rest.dtype)


def embed(embeds, basis, gain, cotangent, after):
    rows, width = embeds.shape
    rank = basis.shape[1]
    vmem = pl.BlockSpec(memory_space=pltpu.VMEM)
    return pl.pallas_call(
        embed_kernel,
        in_specs=[vmem] * 4 + [pl.BlockSpec(memory_space=pl.ANY)],
        out_specs=[vmem] * 7,
        out_shape=[
            jax.ShapeDtypeStruct((rank, rows), F32),
            jax.ShapeDtypeStruct((1, rows), F32),
            jax.ShapeDtypeStruct((rank, rows), BF16),
            jax.ShapeDtypeStruct((rows, width // 2), BF16),
            jax.ShapeDtypeStruct((1, width // 2), F32),
            jax.ShapeDtypeStruct((rows, 1536), BF16),
            jax.ShapeDtypeStruct((rows, width // 2 - 1536 + 3 * rank + 128), BF16),
        ],
        compiler_params=pltpu.CompilerParams(vmem_limit_bytes=16 * 1024 * 1024),
        name="embed",
    )(embeds, basis, gain, cotangent, after)


def join_kernel(part, crossed, out):
    out[0] = part[...]
    out[1] = crossed[...]


def join(part, crossed):
    return pl.pallas_call(
        join_kernel,
        out_shape=jax.ShapeDtypeStruct((2,) + part.shape, part.dtype),
        compiler_params=pltpu.CompilerParams(vmem_limit_bytes=4 * 1024 * 1024),
        name="join",
    )(part, crossed)


def chain_kernel(
    every, norm, emb_basis, cotangent, mine, basis, gain, share_wide, share,
    coefs_hbm, slots,
    turned, links, behind, c_kept, g_kept, p_kept, a_kept, pre_kept, slope_kept, coefs, coefs_sem,
):
    count = 2 * every.shape[0]
    rows, width = mine.shape[0], 2 * mine.shape[1]
    inner = 64
    half = lax.axis_index("z_hi")
    core = lax.axis_index("core")
    me = 2 * lax.axis_index("y") + half
    sides = (half, 1 - half)

    def down_of(s):
        return jnp.concatenate([every[s // 2, k, sides[s % 2], :, :128] for k in range(2)], axis=1)

    def up_of(s):
        return jnp.concatenate([every[s // 2, k, sides[s % 2], :, 128:256] for k in range(2)], axis=1)

    for s in range(count):
        turned[s, 0] = down_of(s).T
        turned[s, 1] = up_of(s).T
    for s in range(1, count):
        links[s, 0] = dot(down_of(s), up_of(s - 1), NT).astype(BF16)
        links[s, 1] = dot(up_of(s - 1), down_of(s), NT).astype(BF16)

    theirs = jnp.concatenate(
        [share[:, at : at + 128].astype(F32) + share[:, at + 256 : at + 384].astype(F32) for at in (512, 640)], axis=0
    )
    parts = share[:16, 1280:1408].astype(F32)
    eu = jnp.concatenate([emb_basis[...], theirs], axis=1)
    sq = jnp.concatenate([norm[...], parts[0:1] + parts[1:2] + parts[2:3]], axis=1)
    c = jnp.zeros(eu.shape, BF16)
    c_kept[0] = c
    invs = []
    base = None
    act = None
    for s in range(count):
        cf = c.astype(F32)
        pre = jnp.concatenate(
            [every[s // 2, k, sides[s % 2], :, 256:].astype(F32) for k in (core, 1 - core)], axis=1
        )
        total = sq
        if s:
            pre = pre + dot(links[s, 0], act)
            if base is not None:
                pre = pre + base
            hid = eu + cf
            total = total + jnp.sum(cf * (eu + hid), axis=0, keepdims=True)
            behind[s] = dot(up_of(s - 1), hid.astype(BF16))
            if s + 1 < count:
                base = dot(down_of(s + 1), c)
        inv = lax.rsqrt(jnp.maximum(total, 0.0) * (1.0 / width) + EPS)
        invs.append(inv)
        pre = pre * inv
        sig = 1.0 / (1.0 + jnp.exp(-pre))
        act = (pre * sig).astype(BF16)
        pre_kept[s] = pre
        slope_kept[s] = sig * (1.0 + pre * (1.0 - sig))
        a_kept[s] = act
        c = (cf + dot(turned[s, 1], act)).astype(BF16)
        c_kept[s + 1] = c
    coefs[...] = c_kept[me + 1, :, :rows].T
    coefs_copy = pltpu.make_async_copy(coefs, coefs_hbm, coefs_sem)
    coefs_copy.start()

    g = jnp.concatenate(
        [cotangent[...], jnp.concatenate([share[:, 1024:1152], share[:, 1152:1280]], axis=0)], axis=1
    )
    grad_act = dot(up_of(count - 1), g)
    for s in reversed(range(count)):
        g_kept[s] = g
        inv = invs[s]
        gp = (grad_act * slope_kept[s]).astype(BF16)
        gpf = gp.astype(F32)
        p_kept[s] = (gpf * inv).astype(BF16)
        if s:
            base = dot(up_of(s - 1), g)
            pull = inv * inv * (jnp.sum(gpf * pre_kept[s], axis=0, keepdims=True) * (1.0 / width))
            grad_act = base + inv * dot(links[s, 1], gp) - pull * behind[s]
            hid = eu + c_kept[s].astype(F32)
            g = (g.astype(F32) + inv * dot(turned[s, 0], gp) - pull * hid).astype(BF16)

    p_t = p_kept[me]
    cp = dot(p_t, c_kept[me], NT).astype(BF16)
    s2 = dot(a_kept[me], g_kept[me], NT).astype(BF16)
    for j in range(8):
        lanes = slice(j * 256, j * 256 + 256)
        rest = share_wide[:, lanes] if j < 6 else share[:, j * 256 - 1536 : j * 256 - 1280]
        tokens = jnp.concatenate([mine[:, lanes], rest], axis=0)
        spans = jnp.concatenate([basis[far, j, core] for far in range(4)], axis=0)
        slots[j, :, :256] = ((dot(p_t, tokens) + dot(cp, spans, NT)) * gain[:, lanes]).astype(BF16)
        slots[j, :, 256:] = s2
    coefs_copy.wait()


def chain(every, norm, emb_basis, cotangent, mine, basis, gain, share_wide, share):
    count = 2 * every.shape[0]
    rank, rows = cotangent.shape
    tokens = 2 * rows
    inner = 64
    hbm = pl.BlockSpec(memory_space=pltpu.HBM)
    vmem = pl.BlockSpec(memory_space=pltpu.VMEM)
    return pl.pallas_call(
        chain_kernel,
        in_specs=[vmem] * 9,
        out_specs=[hbm, vmem],
        out_shape=[
            pltpu.HBM((rows, rank), BF16),
            jax.ShapeDtypeStruct((8, inner, 2 * rank), BF16),
        ],
        scratch_shapes=[
            pltpu.VMEM((count, 2, rank, inner), BF16),
            pltpu.VMEM((count, 2, inner, inner), BF16),
            pltpu.VMEM((count, inner, tokens), F32),
            pltpu.VMEM((count + 1, rank, tokens), BF16),
            pltpu.VMEM((count, rank, tokens), BF16),
            pltpu.VMEM((count, inner, tokens), BF16),
            pltpu.VMEM((count, inner, tokens), BF16),
            pltpu.VMEM((count, inner, tokens), F32),
            pltpu.VMEM((count, inner, tokens), F32),
            pltpu.VMEM((rows, rank), BF16),
            pltpu.SemaphoreType.DMA,
        ],
        compiler_params=pltpu.CompilerParams(vmem_limit_bytes=32 * 1024 * 1024),
        name="chain",
    )(every, norm, emb_basis, cotangent, mine, basis.reshape(4, 8, 2, 64, 256), gain, share_wide, share)


def middle_kernel(got, basis, out):
    total = got[0].astype(F32)
    for j in range(1, got.shape[0]):
        total = total + got[j].astype(F32)
    lane = 4 * lax.axis_index("z_near") + lax.axis_index("x")
    rows = basis[:, lane, lax.axis_index("core")].reshape(256, 256)
    w2 = dot(total[:, 256:].astype(BF16), rows, NT)
    both = jnp.concatenate([total[:, :256], w2], axis=0)
    out[...] = both.T.astype(BF16).reshape(out.shape)


def middle(got, basis):
    return pl.pallas_call(
        middle_kernel,
        in_specs=[pl.BlockSpec(memory_space=pltpu.VMEM)] * 2,
        out_specs=pl.BlockSpec(memory_space=pltpu.VMEM),
        out_shape=jax.ShapeDtypeStruct((4, 64, 128), BF16),
        compiler_params=pltpu.CompilerParams(vmem_limit_bytes=16 * 1024 * 1024),
        name="middle",
    )(got, basis.reshape(4, 8, 2, 64, 256))


def final_kernel(got, out):
    total = got[0].astype(F32)
    for j in range(1, got.shape[0]):
        total = total + got[j].astype(F32)
    out[...] = total


def final(got):
    return pl.pallas_call(
        final_kernel,
        out_shape=jax.ShapeDtypeStruct(got.shape[1:], F32),
        compiler_params=pltpu.CompilerParams(vmem_limit_bytes=4 * 1024 * 1024),
        name="final",
    )(got)


def local(embeds, shared_basis, down_proj, up_proj, norm_gain, coef_grad):
    part = project(embeds, shared_basis, down_proj[0].T, up_proj[0].T, norm_gain)
    crossed = lax.ppermute(part, "z_hi", [(0, 1), (1, 0)])
    emb_basis, norm, cot, mine, gain, share_wide, share = embed(embeds, shared_basis, norm_gain, coef_grad, part)
    share_wide = lax.ppermute(share_wide, "core", [(0, 1), (1, 0)])
    share = lax.ppermute(share, "core", [(0, 1), (1, 0)])
    every = lax.all_gather(join(part, crossed), ("y", "core"), tiled=False)
    every = every.reshape((4, 2, 2) + part.shape)
    coefs, slots = chain(every, norm, emb_basis, cot, mine, shared_basis, gain, share_wide, share)
    got = lax.all_to_all(slots, ("z_near", "x"), 0, 0, tiled=True)
    got = lax.all_to_all(middle(got, shared_basis), "z_far", 0, 0, tiled=True)
    return coefs[None], final(got)[None]


def solution(mesh):
    fine = Mesh(mesh.devices.reshape(SIZES), AXES)
    placed = (
        P(REPLICA, None),
        P(),
        P(SECTION, None, None),
        P(SECTION, None, None),
        P(SECTION, None),
        P(REPLICA, None),
    )
    return jax.shard_map(
        local,
        mesh=fine,
        in_specs=placed,
        out_specs=(P(SECTION, REPLICA, None), P(SECTION, REPLICA, None)),
        check_vma=False,
    )
```

```python
import functools

import jax
import jax.numpy as jnp
from jax import lax
from jax.experimental import pallas as pl
from jax.experimental.pallas import tpu as pltpu
from jax.sharding import Mesh, PartitionSpec as P

F32 = jnp.float32
BF16 = jnp.bfloat16
EPS = 1e-05
SECTION = ("y", "z_hi")
REPLICA = ("z_far", "z_near", "x", "core")
AXES = SECTION + REPLICA
SIZES = (4, 2, 4, 2, 4, 2)

NN = (((1,), (0,)), ((), ()))
NT = (((1,), (1,)), ((), ()))
TN = (((0,), (0,)), ((), ()))


def dot(a, b, dims=NN):
    return lax.dot_general(a, b, dims, preferred_element_type=F32)


def project_kernel(
    sizes, emb_hbm, basis_hbm, down_hbm, up_hbm, gain_hbm,
    part, emb, basis, down, up, gain, sems,
):
    rows, width = emb.shape
    inner = down.shape[0]
    half = pl.ds(pl.multiple_of(lax.axis_index("core") * 128, 128), 128)
    gain_copy = pltpu.make_async_copy(gain_hbm, gain, sems.at[4, 0])
    gain_copy.start()
    spans, copies = [], []
    begin = 0
    for i, size in enumerate(sizes):
        at = slice(begin, begin + size)
        begin += size
        group = [
            pltpu.make_async_copy(basis_hbm.at[at, half], basis.at[at, :], sems.at[3, i]),
            pltpu.make_async_copy(emb_hbm.at[:, at], emb.at[:, at], sems.at[2, i]),
            pltpu.make_async_copy(down_hbm.at[:, at], down.at[:, at], sems.at[0, i]),
            pltpu.make_async_copy(up_hbm.at[:, at], up.at[:, at], sems.at[1, i]),
        ]
        for copy in group:
            copy.start()
        spans.append(at)
        copies.append(group)
    gain_copy.wait()
    acc = jnp.zeros((2 * inner, 128), F32)
    pre = jnp.zeros((inner, rows), F32)
    for at, group in zip(spans, copies):
        for copy in group:
            copy.wait()
        scaled = (down[:, at].astype(F32) * gain[:, at]).astype(BF16)
        acc = acc + dot(jnp.concatenate([scaled, up[:, at]], axis=0), basis[at, :])
        pre = pre + dot(scaled, emb[:, at], NT)
    part[:, :128] = acc[:inner].astype(BF16)
    part[:, 128:256] = acc[inner:].astype(BF16)
    part[:, 256:] = pre.astype(BF16)


def project(embeds, basis, down_t, up_t, gain):
    rows, width = embeds.shape
    rank = basis.shape[1]
    inner = down_t.shape[0]
    sizes = (1024,) * 4
    args = [pltpu.with_memory_space_constraint(a, pltpu.HBM) for a in (embeds, basis, down_t, up_t, gain)]
    return pl.pallas_call(
        functools.partial(project_kernel, sizes),
        in_specs=[pl.BlockSpec(memory_space=pltpu.HBM)] * 5,
        out_specs=pl.BlockSpec(memory_space=pltpu.VMEM),
        out_shape=jax.ShapeDtypeStruct((inner, rank + rows), BF16),
        scratch_shapes=[
            pltpu.VMEM((rows, width), BF16),
            pltpu.VMEM((width, 128), BF16),
            pltpu.VMEM((inner, width), BF16),
            pltpu.VMEM((inner, width), BF16),
            pltpu.VMEM((1, width), F32),
            pltpu.SemaphoreType.DMA((5, len(sizes))),
        ],
        compiler_params=pltpu.CompilerParams(vmem_limit_bytes=24 * 1024 * 1024),
        name="project",
    )(*args)


def embed_kernel(emb, basis, gain, cotangent, after, emb_basis, norm, cot_turned, mine, gain_mine, share_wide, share):
    del after
    rows, width = emb.shape
    chunk = 1024
    acc = jnp.zeros((rows, basis.shape[1]), F32)
    square = jnp.zeros((rows, 128), F32)
    for at in range(0, width, chunk):
        e = emb[:, at : at + chunk]
        acc = acc + dot(e, basis[at : at + chunk, :])
        ef = e.astype(F32)
        sq = ef * ef
        for k in range(0, chunk, 128):
            square = square + sq[:, k : k + 128]
    turned = acc.T
    emb_basis[...] = turned
    high = turned.astype(BF16)
    low_part = (turned - high.astype(F32)).astype(BF16)
    cot = cotangent[...].T
    cot_turned[...] = cot
    for begin, whole in ((512, high), (768, low_part), (1024, cot)):
        share[:, begin : begin + 128] = whole[:rows]
        share[:, begin + 128 : begin + 256] = whole[rows:]
    total = jnp.sum(square.T, axis=0, keepdims=True)
    norm[...] = total
    total = jnp.broadcast_to(total, (rows, 128))
    first = total.astype(BF16).astype(F32)
    second = (total - first).astype(BF16).astype(F32)
    row = lax.broadcasted_iota(jnp.int32, (rows, 128), 0)
    parts = jnp.where(row == 0, first, jnp.where(row == 1, second, total - first - second))
    share[:, 1280:1408] = parts.astype(BF16)
    even = lax.axis_index("core") == 0
    for j in range(8):
        for q in range(2):
            one = slice(2048 * q + j * 128, 2048 * q + j * 128 + 128)
            two = slice(2048 * q + 1024 + j * 128, 2048 * q + 1024 + j * 128 + 128)
            lanes = slice(j * 256 + q * 128, j * 256 + q * 128 + 128)
            for source, target, rest in ((emb, mine, share), (gain, gain_mine, None)):
                left = source[:, one].astype(F32)
                right = source[:, two].astype(F32)
                low = lax.broadcasted_iota(jnp.int32, left.shape, 1) < 64
                zero = jnp.where(low, left, pltpu.roll(right, 64, 1))
                other = jnp.where(low, pltpu.roll(left, 64, 1), right)
                target[:, lanes] = jnp.where(even, zero, other).astype(target.dtype)
                if rest is not None and j < 6:
                    share_wide[:, lanes] = jnp.where(even, other, zero).astype(rest.dtype)
                elif rest is not None:
                    rest[:, lanes.start - 1536 : lanes.stop - 1536] = jnp.where(even, other, zero).astype(rest.dtype)


def embed(embeds, basis, gain, cotangent, after):
    rows, width = embeds.shape
    rank = basis.shape[1]
    vmem = pl.BlockSpec(memory_space=pltpu.VMEM)
    return pl.pallas_call(
        embed_kernel,
        in_specs=[vmem] * 4 + [pl.BlockSpec(memory_space=pl.ANY)],
        out_specs=[vmem] * 7,
        out_shape=[
            jax.ShapeDtypeStruct((rank, rows), F32),
            jax.ShapeDtypeStruct((1, rows), F32),
            jax.ShapeDtypeStruct((rank, rows), BF16),
            jax.ShapeDtypeStruct((rows, width // 2), BF16),
            jax.ShapeDtypeStruct((1, width // 2), F32),
            jax.ShapeDtypeStruct((rows, 1536), BF16),
            jax.ShapeDtypeStruct((rows, width // 2 - 1536 + 3 * rank + 128), BF16),
        ],
        compiler_params=pltpu.CompilerParams(vmem_limit_bytes=16 * 1024 * 1024),
        name="embed",
    )(embeds, basis, gain, cotangent, after)


def join_kernel(part, crossed, out):
    out[0] = part[...]
    out[1] = crossed[...]


def join(part, crossed):
    return pl.pallas_call(
        join_kernel,
        out_shape=jax.ShapeDtypeStruct((2,) + part.shape, part.dtype),
        compiler_params=pltpu.CompilerParams(vmem_limit_bytes=4 * 1024 * 1024),
        name="join",
    )(part, crossed)


def chain_kernel(
    every, norm, emb_basis, cotangent, mine, basis, gain, share_wide, share,
    coefs_hbm, slots,
    turned, links, behind, c_kept, g_kept, p_kept, a_kept, pre_kept, slope_kept, coefs, coefs_sem,
):
    count = 2 * every.shape[0]
    rows, width = mine.shape[0], 2 * mine.shape[1]
    inner = 64
    half = lax.axis_index("z_hi")
    core = lax.axis_index("core")
    me = 2 * lax.axis_index("y") + half
    sides = (half, 1 - half)

    def down_of(s):
        return jnp.concatenate([every[s // 2, k, sides[s % 2], :, :128] for k in range(2)], axis=1)

    def up_of(s):
        return jnp.concatenate([every[s // 2, k, sides[s % 2], :, 128:256] for k in range(2)], axis=1)

    for s in range(count):
        turned[s, 0] = down_of(s).T
        turned[s, 1] = up_of(s).T
    for s in range(1, count):
        links[s, 0] = dot(down_of(s), up_of(s - 1), NT).astype(BF16)
        links[s, 1] = dot(up_of(s - 1), down_of(s), NT).astype(BF16)

    theirs = jnp.concatenate(
        [share[:, at : at + 128].astype(F32) + share[:, at + 256 : at + 384].astype(F32) for at in (512, 640)], axis=0
    )
    parts = share[:16, 1280:1408].astype(F32)
    eu = jnp.concatenate([emb_basis[...], theirs], axis=1)
    sq = jnp.concatenate([norm[...], parts[0:1] + parts[1:2] + parts[2:3]], axis=1)
    c = jnp.zeros(eu.shape, BF16)
    c_kept[0] = c
    invs = []
    base = None
    act = None
    for s in range(count):
        cf = c.astype(F32)
        pre = jnp.concatenate(
            [every[s // 2, k, sides[s % 2], :, 256:].astype(F32) for k in (core, 1 - core)], axis=1
        )
        total = sq
        if s:
            pre = pre + dot(links[s, 0], act)
            if base is not None:
                pre = pre + base
            hid = eu + cf
            total = total + jnp.sum(cf * (eu + hid), axis=0, keepdims=True)
            behind[s] = dot(up_of(s - 1), hid.astype(BF16))
            if s + 1 < count:
                base = dot(down_of(s + 1), c)
        inv = lax.rsqrt(jnp.maximum(total, 0.0) * (1.0 / width) + EPS)
        invs.append(inv)
        pre = pre * inv
        sig = 0.5 + 0.5 * jnp.tanh(0.5 * pre)
        act = (pre * sig).astype(BF16)
        pre_kept[s] = pre
        slope_kept[s] = sig * (1.0 + pre * (1.0 - sig))
        a_kept[s] = act
        c = (cf + dot(turned[s, 1], act)).astype(BF16)
        c_kept[s + 1] = c
    coefs[...] = c_kept[me + 1, :, :rows].T
    coefs_copy = pltpu.make_async_copy(coefs, coefs_hbm, coefs_sem)
    coefs_copy.start()

    g = jnp.concatenate(
        [cotangent[...], jnp.concatenate([share[:, 1024:1152], share[:, 1152:1280]], axis=0)], axis=1
    )
    grad_act = dot(up_of(count - 1), g)
    for s in reversed(range(count)):
        g_kept[s] = g
        inv = invs[s]
        gp = (grad_act * slope_kept[s]).astype(BF16)
        gpf = gp.astype(F32)
        p_kept[s] = (gpf * inv).astype(BF16)
        if s:
            base = dot(up_of(s - 1), g)
            pull = inv * inv * (jnp.sum(gpf * pre_kept[s], axis=0, keepdims=True) * (1.0 / width))
            grad_act = base + inv * dot(links[s, 1], gp) - pull * behind[s]
            hid = eu + c_kept[s].astype(F32)
            g = (g.astype(F32) + inv * dot(turned[s, 0], gp) - pull * hid).astype(BF16)

    p_t = p_kept[me]
    cp = dot(p_t, c_kept[me], NT).astype(BF16)
    s2 = dot(a_kept[me], g_kept[me], NT).astype(BF16)
    for j in range(8):
        lanes = slice(j * 256, j * 256 + 256)
        rest = share_wide[:, lanes] if j < 6 else share[:, j * 256 - 1536 : j * 256 - 1280]
        tokens = jnp.concatenate([mine[:, lanes], rest], axis=0)
        spans = jnp.concatenate([basis[far, j, core] for far in range(4)], axis=0)
        slots[j, :, :256] = ((dot(p_t, tokens) + dot(cp, spans, NT)) * gain[:, lanes]).astype(BF16)
        slots[j, :, 256:] = s2
    coefs_copy.wait()


def chain(every, norm, emb_basis, cotangent, mine, basis, gain, share_wide, share):
    count = 2 * every.shape[0]
    rank, rows = cotangent.shape
    tokens = 2 * rows
    inner = 64
    hbm = pl.BlockSpec(memory_space=pltpu.HBM)
    vmem = pl.BlockSpec(memory_space=pltpu.VMEM)
    return pl.pallas_call(
        chain_kernel,
        in_specs=[vmem] * 9,
        out_specs=[hbm, vmem],
        out_shape=[
            pltpu.HBM((rows, rank), BF16),
            jax.ShapeDtypeStruct((8, inner, 2 * rank), BF16),
        ],
        scratch_shapes=[
            pltpu.VMEM((count, 2, rank, inner), BF16),
            pltpu.VMEM((count, 2, inner, inner), BF16),
            pltpu.VMEM((count, inner, tokens), F32),
            pltpu.VMEM((count + 1, rank, tokens), BF16),
            pltpu.VMEM((count, rank, tokens), BF16),
            pltpu.VMEM((count, inner, tokens), BF16),
            pltpu.VMEM((count, inner, tokens), BF16),
            pltpu.VMEM((count, inner, tokens), F32),
            pltpu.VMEM((count, inner, tokens), F32),
            pltpu.VMEM((rows, rank), BF16),
            pltpu.SemaphoreType.DMA,
        ],
        compiler_params=pltpu.CompilerParams(vmem_limit_bytes=32 * 1024 * 1024),
        name="chain",
    )(every, norm, emb_basis, cotangent, mine, basis.reshape(4, 8, 2, 64, 256), gain, share_wide, share)


def middle_kernel(got, basis, out):
    total = got[0].astype(F32)
    for j in range(1, got.shape[0]):
        total = total + got[j].astype(F32)
    lane = 4 * lax.axis_index("z_near") + lax.axis_index("x")
    rows = basis[:, lane, lax.axis_index("core")].reshape(256, 256)
    w2 = dot(total[:, 256:].astype(BF16), rows, NT)
    both = jnp.concatenate([total[:, :256], w2], axis=0)
    out[...] = both.T.astype(BF16).reshape(out.shape)


def middle(got, basis):
    return pl.pallas_call(
        middle_kernel,
        in_specs=[pl.BlockSpec(memory_space=pltpu.VMEM)] * 2,
        out_specs=pl.BlockSpec(memory_space=pltpu.VMEM),
        out_shape=jax.ShapeDtypeStruct((4, 64, 128), BF16),
        compiler_params=pltpu.CompilerParams(vmem_limit_bytes=16 * 1024 * 1024),
        name="middle",
    )(got, basis.reshape(4, 8, 2, 64, 256))


def final_kernel(got, out):
    total = got[0].astype(F32)
    for j in range(1, got.shape[0]):
        total = total + got[j].astype(F32)
    out[...] = total


def final(got):
    return pl.pallas_call(
        final_kernel,
        out_shape=jax.ShapeDtypeStruct(got.shape[1:], F32),
        compiler_params=pltpu.CompilerParams(vmem_limit_bytes=4 * 1024 * 1024),
        name="final",
    )(got)


def local(embeds, shared_basis, down_proj, up_proj, norm_gain, coef_grad):
    part = project(embeds, shared_basis, down_proj[0].T, up_proj[0].T, norm_gain)
    crossed = lax.ppermute(part, "z_hi", [(0, 1), (1, 0)])
    emb_basis, norm, cot, mine, gain, share_wide, share = embed(embeds, shared_basis, norm_gain, coef_grad, part)
    share_wide = lax.ppermute(share_wide, "core", [(0, 1), (1, 0)])
    share = lax.ppermute(share, "core", [(0, 1), (1, 0)])
    every = lax.all_gather(join(part, crossed), ("y", "core"), tiled=False)
    every = every.reshape((4, 2, 2) + part.shape)
    coefs, slots = chain(every, norm, emb_basis, cot, mine, shared_basis, gain, share_wide, share)
    got = lax.all_to_all(slots, ("z_near", "x"), 0, 0, tiled=True)
    got = lax.all_to_all(middle(got, shared_basis), "z_far", 0, 0, tiled=True)
    return coefs[None], final(got)[None]


def solution(mesh):
    fine = Mesh(mesh.devices.reshape(SIZES), AXES)
    placed = (
        P(REPLICA, None),
        P(),
        P(SECTION, None, None),
        P(SECTION, None, None),
        P(SECTION, None),
        P(REPLICA, None),
    )
    return jax.shard_map(
        local,
        mesh=fine,
        in_specs=placed,
        out_specs=(P(SECTION, REPLICA, None), P(SECTION, REPLICA, None)),
        check_vma=False,
    )
```
